128 devices in a mesh: group: 8 (over z, y_lo), proc: 16 (over x, y_hi, core).
Axes of the slice: x: 4, y: 4 (y_hi: 2, y_lo: 2; y = y_hi * 2 + y_lo), z: 4, core: 2. Of those that a mesh axis runs over, the one named last changes fastest.
Arguments:
- pattern: int32 [34], replicated, may hold values 0 or 1
- inverse_root: float32 [2, 768, 768], P(None, 'proc'), may hold values from -1.5 to 1.5, as said below
- inverse_one: float32 [2, 768, 1536], P(None, 'proc', 'group'), may hold values from -1.5 to 1.5, as said below
- inverse_two: float32 [2, 768, 3072], P(None, 'proc', 'group'), may hold values from -1.5 to 1.5, as said below
- inverse_three: float32 [2, 768, 6144], P(None, 'proc', 'group'), may hold values from -1.5 to 1.5, as said below
- lower_one: float32 [2, 1, 768, 1536], P(None, None, 'proc', 'group'), may hold values from -0.15625 to 0.15625
- lower_two: float32 [2, 2, 768, 3072], P(None, None, 'proc', 'group'), may hold values from -0.15625 to 0.15625
- lower_three: float32 [2, 3, 768, 6144], P(None, None, 'proc', 'group'), may hold values from -0.15625 to 0.15625
Outputs:
- upper_one: float32 [2, 1, 768, 1536], P(None, None, 'proc', 'group')
- upper_two: float32 [2, 2, 768, 3072], P(None, None, 'proc', 'group')
- upper_three: float32 [2, 3, 768, 6144], P(None, None, 'proc', 'group')
- diagonal_one: float32 [2, 768, 1536], P(None, 'proc', 'group')
- diagonal_two: float32 [2, 768, 3072], P(None, 'proc', 'group')
- diagonal_three: float32 [2, 768, 6144], P(None, 'proc', 'group')
The draws below stay inside these ranges and needn't reach their ends.
Inputs may be any that keep to these rules, and one draw needn't show every extreme that they name: `inverse_root`: each 768 by 768 block along the last dimension is symmetric in both parts. `inverse_one`: each 768 by 768 block along the last dimension is symmetric in both parts. `inverse_two`: each 768 by 768 block along the last dimension is symmetric in both parts. `inverse_three`: each 768 by 768 block along the last dimension is symmetric in both parts.
All inputs are finite; a program needn't handle non-finite values.
Results may differ from the reference program's by a relative error of at most 0.0002.
Values sent between devices are 32-bit elements; how exact they have to be, the bound alone decides.
A program may use at most 128 MiB of HBM per device.

```python
import math
import jax
import jax.numpy as jnp
from jax import lax

S = 768


def symmetric_blocks(key, block_count):
    key_normal = jax.random.fold_in(key, 0)
    key_real = jax.random.fold_in(key, 2)
    key_imag = jax.random.fold_in(key, 3)
    normal_part = jax.random.truncated_normal(key_normal, -4.0, 4.0, (2, block_count, S, S), jnp.float32)
    raw_offdiag = normal_part
    mirrored = (raw_offdiag + jnp.swapaxes(raw_offdiag, 2, 3)) * (0.5 / math.sqrt(S))
    identity = jnp.eye(S, dtype=jnp.float32)
    real_diag = jax.random.uniform(key_real, (block_count, S), jnp.float32, 0.6, 1.4)
    imag_diag = jax.random.uniform(key_imag, (block_count, S), jnp.float32, -0.6, 0.6)
    diag_values = jnp.stack([real_diag, imag_diag])
    blocks = mirrored * (1.0 - identity) + diag_values[..., None] * identity
    return blocks.transpose(0, 2, 1, 3).reshape(2, S, block_count * S)


def draw_inverse_root(key, part):
    key = jax.random.fold_in(key, 11)
    return symmetric_blocks(key, 1)


def draw_inverse_one(key, part):
    key = jax.random.fold_in(key, 12)
    return symmetric_blocks(key, 2)


def draw_inverse_two(key, part):
    key = jax.random.fold_in(key, 13)
    return symmetric_blocks(key, 4)


def draw_inverse_three(key, part):
    key = jax.random.fold_in(key, 14)
    return symmetric_blocks(key, 8)


def touch_ends(array, stream_key, least, top_value):
    index_at = [jax.random.randint(jax.random.fold_in(stream_key, axis), (), 0, length) for axis, length in enumerate(array.shape)]
    main_axis = array.shape.index(max(array.shape))
    neighbour = index_at[:main_axis] + [(index_at[main_axis] + 1) % array.shape[main_axis]] + index_at[main_axis + 1:]
    return array.at[tuple(index_at)].set(least).at[tuple(neighbour)].set(top_value)


def shard_levels(own_key, dims, shards, smallest, top_value):
    factor_of, own = 1.0, jax.random.fold_in(own_key, 6)
    for dim, blocks in shards:
        draws = jnp.exp(jax.random.uniform(jax.random.fold_in(own, dim), (blocks,), jnp.float32, smallest / len(shards), top_value / len(shards)))
        factor_of = factor_of * jnp.repeat(draws, dims[dim] // blocks).reshape([-1 if axis == dim else 1 for axis in range(len(dims))])
    return factor_of


def normal_values(stream_key, shape, deviation, bound, pieces=(), held_as=jnp.bfloat16):
    entries = jax.random.normal(stream_key, shape, jnp.float32) * deviation
    if len(pieces) > 0:
        entries = shard_levels(stream_key, shape, pieces, -0.22, 0.18) * entries
    return jnp.clip(entries, min=-bound, max=bound).astype(held_as)


def setup_inputs(seed: int = 0) -> dict:
    arg_keys = jax.random.split(jax.random.key(seed), 9)
    return {
        "pattern": touch_ends((jax.random.randint(arg_keys[0], (34,), 0, 4) < 3).astype(jnp.int32), jax.random.fold_in(arg_keys[0], 1), 0, 1),
        "inverse_root": draw_inverse_root(jax.random.fold_in(arg_keys[8], 71), 0),
        "inverse_one": draw_inverse_one(jax.random.fold_in(arg_keys[8], 71), 0),
        "inverse_two": draw_inverse_two(jax.random.fold_in(arg_keys[8], 71), 0),
        "inverse_three": draw_inverse_three(jax.random.fold_in(arg_keys[8], 71), 0),
        "lower_one": normal_values(arg_keys[5], (2, 1, S, 2 * S), (2 * S) ** -0.5, 0.15625, ((2, 16), (3, 8)), jnp.float32),
        "lower_two": normal_values(arg_keys[6], (2, 2, S, 4 * S), (2 * S) ** -0.5, 0.15625, ((2, 16), (3, 8)), jnp.float32),
        "lower_three": normal_values(arg_keys[7], (2, 3, S, 8 * S), (2 * S) ** -0.5, 0.15625, ((2, 16), (3, 8)), jnp.float32),
    }


def complex_product(left, right):
    def product(first, second):
        return jnp.dot(first, second, precision=lax.Precision.HIGHEST, preferred_element_type=jnp.float32)
    real_part = product(left[0], right[0]) - product(left[1], right[1])
    imag_part = product(left[0], right[1]) + product(left[1], right[0])
    return jnp.stack([real_part, imag_part])


def flip_block(matrix):
    return jnp.swapaxes(matrix, 1, 2)


def pick_block(diagonal_map, upper_map, x, y):
    if x == y:
        return diagonal_map[x]
    if x[0] < y[0]:
        return upper_map[(x, y)]
    return flip_block(upper_map[(y, x)])


def reference(pattern, inverse_root, inverse_one, inverse_two, inverse_three, lower_one, lower_two, lower_three):
    node_width = inverse_root.shape[1]
    inverses = [inverse_root, inverse_one, inverse_two, inverse_three]
    lowers = [None, lower_one, lower_two, lower_three]
    diagonal_map = {(0, 0): inverse_root}
    upper_map = {}
    upper_outs = []
    diag_outs = []
    for level_at in (1, 2, 3):
        first_entry = (level_at - 2) * 2 ** level_at + 2
        upper_list = []
        diag_list = []
        for node_at in range(2 ** level_at):
            ancestors = [(a, node_at >> (level_at - a)) for a in range(level_at)]
            row_blocks = []
            for x in ancestors:
                row_blocks.append(jnp.concatenate([pick_block(diagonal_map, upper_map, x, y) for y in ancestors], axis=2))
            chain_mat = jnp.concatenate(row_blocks, axis=1)
            col_begin = node_at * node_width
            lower_blocks = [lowers[level_at][:, a, :, col_begin:col_begin + node_width] * pattern[first_entry + node_at * level_at + a].astype(jnp.float32) for a in range(level_at)]
            lower_col = jnp.concatenate(lower_blocks, axis=1)
            upper_col = -complex_product(chain_mat, lower_col)
            diag_block = inverses[level_at][:, :, col_begin:col_begin + node_width] - complex_product(flip_block(lower_col), upper_col)
            for a in range(level_at):
                upper_map[(ancestors[a], (level_at, node_at))] = upper_col[:, a * node_width:(a + 1) * node_width]
            diagonal_map[(level_at, node_at)] = diag_block
            upper_list.append(upper_col.reshape(2, level_at, node_width, node_width))
            diag_list.append(diag_block)
        upper_outs.append(jnp.concatenate(upper_list, axis=3))
        diag_outs.append(jnp.concatenate(diag_list, axis=2))
    return (upper_outs[0], upper_outs[1], upper_outs[2], diag_outs[0], diag_outs[1], diag_outs[2])
```

```python
import jax
import jax.numpy as jnp
from jax import lax
from jax.experimental import pallas as pl
from jax.experimental.pallas import tpu as pltpu
from jax.sharding import PartitionSpec as P

MESH = pl.DeviceIdType.MESH
S = 768
PROCS = 16
ROWS = S // PROCS
HALF = ROWS // 2
CHUNKS = 3
WIDTH = S // CHUNKS
WIDE = (256, 384)
COLS = (192, 384)
ROLES = 32


def split(value):
    high = value.astype(jnp.bfloat16)
    low = (value - high.astype(jnp.float32)).astype(jnp.bfloat16)
    return high, low


def dot(first, second):
    return jnp.dot(first, second, preferred_element_type=jnp.float32)


def complex_rows(high, low, real_high, real_low, imag_high, imag_low):
    both = high.shape[0]
    half = both // 2
    stacked = jnp.concatenate([high, low], axis=0)
    by_real = dot(stacked, real_high)
    by_real = by_real[:both] + by_real[both:] + dot(high, real_low)
    by_imag = dot(stacked, imag_high)
    by_imag = by_imag[:both] + by_imag[both:] + dot(high, imag_low)
    return by_real[:half] - by_imag[half:], by_imag[:half] + by_real[half:]


def kernel(
    pattern,
    inverse_root,
    inverse_one,
    inverse_two,
    inverse_three,
    lower_one,
    lower_two,
    lower_three,
    upper_one,
    upper_two,
    upper_three,
    diagonal_one,
    diagonal_two,
    diagonal_three,
    full_one,
    full_two,
    full_three,
    high_one,
    high_two,
    high_three,
    low_one,
    low_two,
    low_three,
    chain,
    join_one,
    join_two,
    joined,
    join_diag_one,
    join_diag_two,
    send_one,
    send_two,
    send_three,
    turned_one,
    turned_two,
    turned_three,
    gather_send,
    gather_recv,
    join_send,
    join_recv,
    turn_send,
    turn_recv,
):
    group = lax.axis_index("group")
    me = lax.axis_index("proc")
    x_at = me // 4
    y_at = me // 2 % 2
    core = me % 2

    def proc_of(dx, dy, dc=0):
        return lax.rem(x_at + dx, 4) * 4 + lax.rem(y_at + dy, 2) * 2 + lax.rem(core + dc, 2)

    right, left = proc_of(1, 0), proc_of(3, 0)
    far, pair, sibling = proc_of(2, 0), proc_of(0, 1), proc_of(0, 0, 1)
    pair_right, pair_left, pair_far = proc_of(1, 1), proc_of(3, 1), proc_of(2, 1)

    barrier = pltpu.get_barrier_semaphore()
    for step in range(1, PROCS):
        pl.semaphore_signal(
            barrier, inc=1, device_id=(group, lax.rem(me + step, PROCS)), device_id_type=MESH
        )
    for flip in range(1, 4):
        pl.semaphore_signal(barrier, inc=1, device_id=(group ^ flip, me), device_id_type=MESH)

    def keep(level, a):
        node = group // 2 ** (3 - level)
        first = (level - 2) * 2**level + 2
        return pattern[first + node * level + a].astype(jnp.float32)

    buffers = [full_one, full_two] + [full_three.at[c] for c in range(CHUNKS)]
    highs = [high_one, high_two] + [high_three.at[c] for c in range(CHUNKS)]
    lows = [low_one, low_two] + [low_three.at[c] for c in range(CHUNKS)]

    def rows_of(proc, offset=0):
        return pl.multiple_of(proc * ROWS + offset, 8)

    own = pl.ds(rows_of(me), ROWS)
    full_one[:, :, own, :] = jnp.zeros((2, 1, ROWS, WIDE[0]), jnp.float32)
    full_one[:, 0, own, : COLS[0]] = lower_one[:, 0] * keep(1, 0)
    for a in range(2):
        full_two[:, a, own, :] = lower_two[:, a] * keep(2, a)
    for a in range(3):
        for c in range(CHUNKS):
            full_three[c, :, a, own, :] = (
                lower_three[:, a, :, c * WIDTH : (c + 1) * WIDTH] * keep(3, a)
            )
    for part in range(2):
        high, low = split(inverse_root[part])
        chain[0, part, 0, :, :S] = high
        chain[1, part, 0, :, :S] = low

    pl.semaphore_wait(barrier, PROCS - 1 + 3)

    pending = []

    def send(chunk, role, part, proc, to, half=None):
        offset, count = (0, ROWS) if half is None else (half * HALF, HALF)
        rows = pl.ds(rows_of(proc, offset), count)
        parts = slice(None) if part is None else slice(part, part + 1)
        place = buffers[chunk].at[parts, :, rows, :]
        copy = pltpu.make_async_remote_copy(
            src_ref=place,
            dst_ref=place,
            send_sem=gather_send.at[chunk, role],
            recv_sem=gather_recv.at[chunk, role],
            device_id=(group, to),
            device_id_type=MESH,
        )
        copy.start()
        pending.append(copy)

    def arrive(chunk, role, part, proc, half=None):
        offset, count = (0, ROWS) if half is None else (half * HALF, HALF)
        rows = pl.ds(rows_of(proc, offset), count)
        parts = slice(None) if part is None else slice(part, part + 1)
        place = buffers[chunk].at[parts, :, rows, :]
        pltpu.make_async_remote_copy(
            src_ref=place,
            dst_ref=place,
            send_sem=gather_send.at[chunk, role],
            recv_sem=gather_recv.at[chunk, role],
            device_id=(group, sibling),
            device_id_type=MESH,
        ).wait_recv()

    def stage_a(q):
        send(q, 0, 0, me, pair)
        send(q, 9, 1, me, right)
        send(q, 10, 1, me, left)
        send(q, 1, 0, me, right)
        send(q, 2, 0, me, left)
        send(q, 13, 1, me, pair)
        send(q, 17, None, me, sibling)

    def stage_b(q):
        arrive(q, 0, 0, pair)
        send(q, 3, 0, pair, right)
        send(q, 4, 0, pair, left)
        send(q, 18, 0, pair, sibling)
        arrive(q, 9, 1, left)
        send(q, 11, 1, left, right, 0)
        send(q, 14, 1, left, pair)
        send(q, 25, 1, left, sibling)
        arrive(q, 10, 1, right)
        send(q, 12, 1, right, left, 1)
        send(q, 15, 1, right, pair)
        send(q, 26, 1, right, sibling)
        arrive(q, 1, 0, left)
        send(q, 5, 0, left, right, 0)
        send(q, 19, 0, left, sibling)
        arrive(q, 2, 0, right)
        send(q, 6, 0, right, left, 1)
        send(q, 20, 0, right, sibling)

    def stage_c(q):
        arrive(q, 11, 1, far, 0)
        arrive(q, 12, 1, far, 1)
        send(q, 16, 1, far, pair)
        send(q, 27, 1, far, sibling)
        arrive(q, 3, 0, pair_left)
        send(q, 7, 0, pair_left, right, 0)
        send(q, 21, 0, pair_left, sibling)
        arrive(q, 4, 0, pair_right)
        send(q, 8, 0, pair_right, left, 1)
        send(q, 22, 0, pair_right, sibling)

    def stage_d(q):
        arrive(q, 13, 1, pair)
        send(q, 28, 1, pair, sibling)
        arrive(q, 5, 0, far, 0)
        arrive(q, 6, 0, far, 1)
        send(q, 23, 0, far, sibling)
        arrive(q, 14, 1, pair_left)
        send(q, 29, 1, pair_left, sibling)
        arrive(q, 15, 1, pair_right)
        send(q, 30, 1, pair_right, sibling)
        arrive(q, 7, 0, pair_far, 0)
        arrive(q, 8, 0, pair_far, 1)
        send(q, 24, 0, pair_far, sibling)
        arrive(q, 16, 1, pair_far)
        send(q, 31, 1, pair_far, sibling)

    def stage_e(q):
        flip = 1 - 2 * core
        arrive(q, 17, None, sibling)
        for role, part, proc in (
            (18, 0, pair),
            (25, 1, left),
            (26, 1, right),
            (19, 0, left),
            (20, 0, right),
            (27, 1, far),
            (21, 0, pair_left),
            (22, 0, pair_right),
            (28, 1, pair),
            (23, 0, far),
            (29, 1, pair_left),
            (30, 1, pair_right),
            (24, 0, pair_far),
            (31, 1, pair_far),
        ):
            arrive(q, role, part, proc + flip)

    def convert(q):
        for part in range(2):
            for a in range(buffers[q].shape[1]):
                high, low = split(buffers[q][part, a])
                highs[q][part, a] = high
                lows[q][part, a] = low

    def factors(q):
        levels, width = highs[q].shape[1], highs[q].shape[3]
        return [
            ref[part].reshape(levels * S, width) for part in range(2) for ref in (highs[q], lows[q])
        ]

    def new_upper(q, level):
        depth = level * S
        rows = 2 * level * ROWS
        high = chain[0, :, :level, :, :depth].reshape(rows, depth)
        low = chain[1, :, :level, :, :depth].reshape(rows, depth)
        real, imag = complex_rows(high, low, *factors(q))
        shape = (level, ROWS, highs[q].shape[3])
        return -real.reshape(shape), -imag.reshape(shape)

    def join_copies(step, flips, ref, slot):
        copies = []
        for flip in flips:
            copy = pltpu.make_async_remote_copy(
                src_ref=ref.at[slot],
                dst_ref=ref.at[slot],
                send_sem=join_send.at[step, flip],
                recv_sem=join_recv.at[step, flip],
                device_id=(group ^ flip, me),
                device_id_type=MESH,
            )
            copy.start()
            copies.append(copy)
        pending.extend(copies)

    def join_waits(step, flips, ref, slot):
        for flip in flips:
            place = ref.at[slot ^ flip]
            pltpu.make_async_remote_copy(
                src_ref=place,
                dst_ref=place,
                send_sem=join_send.at[step, flip],
                recv_sem=join_recv.at[step, flip],
                device_id=(group ^ flip, me),
                device_id_type=MESH,
            ).wait_recv()

    def widen(pieces):
        lane = lax.broadcasted_iota(jnp.int32, (pieces[0].shape[0], 128), 1)
        tiles = []
        for even, odd in ((pieces[0], pieces[1]), (pieces[2], pieces[3])):
            rolled = pltpu.roll(odd, 64, 1)
            tiles += [
                even[:, :128],
                jnp.where(lane < 64, even[:, 128:], rolled[:, :128]),
                rolled[:, 128:],
            ]
        return jnp.concatenate(tiles, axis=1)

    def window(real, imag, proc, base=0):
        start = proc * ROWS - base
        tile, shift = start // 128 * 128, start % 128
        count = 128 if shift + ROWS <= 128 else 256
        lane = lax.broadcasted_iota(jnp.int32, (real.shape[0], 128), 1)
        first = real[:, tile : tile + count]
        second = imag[:, tile : tile + count]
        if shift:
            first = pltpu.roll(first, count - shift, 1)[:, :128]
        if shift != ROWS:
            second = pltpu.roll(second, (count + ROWS - shift) % count, 1)[:, :128]
        return jnp.where(lane < ROWS, first[:, :128], second[:, :128])

    def turn_copy(level, source, target, to):
        return pltpu.make_async_remote_copy(
            src_ref=source.at[to],
            dst_ref=target.at[:, own, :],
            send_sem=turn_send.at[level - 1, to],
            recv_sem=turn_recv.at[level - 1, me],
            device_id=(group, to),
            device_id_type=MESH,
        )

    def turn_arrive(level, source, target, proc):
        pltpu.make_async_remote_copy(
            src_ref=source.at[proc],
            dst_ref=target.at[:, pl.ds(rows_of(proc), ROWS), :],
            send_sem=turn_send.at[level - 1, proc],
            recv_sem=turn_recv.at[level - 1, proc],
            device_id=(group, proc),
            device_id_type=MESH,
        ).wait_recv()

    def turn_start(level, source, target):
        real = joined[0, :level].reshape(level * ROWS, S)
        imag = joined[1, :level].reshape(level * ROWS, S)
        for proc in range(PROCS):
            source[proc] = window(real, imag, proc).reshape(level, ROWS, 128)
        for step in range(1, PROCS):
            copy = turn_copy(level, source, target, lax.rem(me + step, PROCS))
            copy.start()
            pending.append(copy)
        target[:, own, :] = source[me]

    def turn_finish(level, source, target):
        for step in range(1, PROCS):
            turn_arrive(level, source, target, lax.rem(me + PROCS - step, PROCS))
        flat = target[...].reshape(level * S, 128)
        return split(flat.T[: 2 * ROWS])

    def new_diagonal(q, row_high, row_low):
        return complex_rows(row_high, row_low, *factors(q))

    def put_chain(part, a, columns, value):
        high, low = split(value)
        chain[0, part, a, :, columns] = high
        chain[1, part, a, :, columns] = low

    slot_one, slot_two = lax.rem(group, 4), lax.rem(group, 2)
    flips_one, flips_two = (1, 2, 3), (1,)

    stage_a(0)
    stage_a(1)
    stage_b(0)
    stage_c(0)
    stage_d(0)
    stage_e(0)
    convert(0)
    real, imag = new_upper(0, 1)
    for part, value in ((0, real), (1, imag)):
        upper_one[part] = value[:, :, : COLS[0]]
        join_one[slot_one, part] = value[0]
    join_copies(0, flips_one, join_one, slot_one)
    stage_b(1)
    stage_a(2)
    join_waits(0, flips_one, join_one, slot_one)
    for part in range(2):
        value = widen([join_one[j, part] for j in range(4)])
        joined[part, 0] = value
        put_chain(part, 0, slice(S, 2 * S), value)
    turn_start(1, send_one, turned_one)
    stage_c(1)
    row_high, row_low = turn_finish(1, send_one, turned_one)
    for part in range(2):
        rows = slice(part * ROWS, (part + 1) * ROWS)
        chain[0, part, 1, :, :S] = row_high[rows]
        chain[1, part, 1, :, :S] = row_low[rows]
    product = new_diagonal(0, row_high, row_low)
    for part in range(2):
        value = inverse_one[part] - product[part][:, : COLS[0]]
        diagonal_one[part] = value
        join_diag_one[slot_one, part, :, : COLS[0]] = value
    join_copies(1, flips_one, join_diag_one, slot_one)
    stage_d(1)
    join_waits(1, flips_one, join_diag_one, slot_one)
    for part in range(2):
        value = widen([join_diag_one[j, part] for j in range(4)])
        put_chain(part, 1, slice(S, 2 * S), value)

    stage_e(1)
    convert(1)
    real, imag = new_upper(1, 2)
    for part, value in ((0, real), (1, imag)):
        upper_two[part] = value
        join_two[slot_two, part] = value
    join_copies(2, flips_two, join_two, slot_two)
    stage_b(2)
    stage_a(3)
    join_waits(2, flips_two, join_two, slot_two)
    for part in range(2):
        for j in range(2):
            columns = slice(j * COLS[1], (j + 1) * COLS[1])
            for a in range(2):
                value = join_two[j, part, a]
                joined[part, a, :, columns] = value
                put_chain(part, a, slice(2 * S + j * COLS[1], 2 * S + (j + 1) * COLS[1]), value)
    turn_start(2, send_two, turned_two)
    stage_c(2)
    row_high, row_low = turn_finish(2, send_two, turned_two)
    for part in range(2):
        rows = slice(part * ROWS, (part + 1) * ROWS)
        chain[0, part, 2, :, : 2 * S] = row_high[rows]
        chain[1, part, 2, :, : 2 * S] = row_low[rows]
    product = new_diagonal(1, row_high, row_low)
    for part in range(2):
        value = inverse_two[part] - product[part]
        diagonal_two[part] = value
        join_diag_two[slot_two, part] = value
    join_copies(3, flips_two, join_diag_two, slot_two)
    stage_d(2)
    stage_b(3)
    stage_a(4)
    join_waits(3, flips_two, join_diag_two, slot_two)
    for part in range(2):
        for j in range(2):
            put_chain(
                part,
                2,
                slice(2 * S + j * COLS[1], 2 * S + (j + 1) * COLS[1]),
                join_diag_two[j, part],
            )

    done = 0
    for c in range(CHUNKS):
        q = 2 + c
        if c == 1:
            stage_c(4)
        if c == 2:
            stage_d(4)
        stage_e(q)
        convert(q)
        real, imag = new_upper(q, 3)
        columns = slice(c * WIDTH, (c + 1) * WIDTH)
        for part, value in ((0, real), (1, imag)):
            upper_three[part, :, :, columns] = value
            joined[part, :, :, columns] = value
        ready = (c + 1) * WIDTH // ROWS
        for proc in range(done, ready):
            real = joined[0].reshape(3 * ROWS, S)
            imag = joined[1].reshape(3 * ROWS, S)
            send_three[proc] = window(real, imag, proc).reshape(3, ROWS, 128)

            @pl.when(me != proc)
            def _():
                turn_copy(3, send_three, turned_three, proc).start()

        done = ready
        if c == 0:
            stage_c(3)
            stage_d(3)
            stage_b(4)
    turned_three[:, own, :] = send_three[me]
    row_high, row_low = turn_finish(3, send_three, turned_three)
    for c in range(CHUNKS):
        columns = slice(c * WIDTH, (c + 1) * WIDTH)
        product = new_diagonal(2 + c, row_high, row_low)
        for part in range(2):
            diagonal_three[part, :, columns] = inverse_three[part, :, columns] - product[part]

    for copy in pending:
        copy.wait_send()
    for step in range(1, PROCS):
        turn_copy(3, send_three, turned_three, lax.rem(me + step, PROCS)).wait_send()


def shards(*arguments):
    f32, bf16 = jnp.float32, jnp.bfloat16
    outputs = [jax.ShapeDtypeStruct(a.shape, f32) for a in arguments[5:8] + arguments[2:5]]
    vmem = pl.BlockSpec(memory_space=pltpu.VMEM)
    fulls = [(2, 1, S, WIDE[0]), (2, 2, S, WIDE[1]), (CHUNKS, 2, 3, S, WIDTH)]
    sends = [(PROCS, level, ROWS, 128) for level in (1, 2, 3)]
    turns = [(level, S, 128) for level in (1, 2, 3)]
    return pl.pallas_call(
        kernel,
        out_shape=outputs,
        in_specs=[pl.BlockSpec(memory_space=pltpu.SMEM)] + [vmem] * 7,
        out_specs=[vmem] * 6,
        scratch_shapes=[pltpu.VMEM(shape, f32) for shape in fulls]
        + [pltpu.VMEM(shape, bf16) for shape in fulls]
        + [pltpu.VMEM(shape, bf16) for shape in fulls]
        + [
            pltpu.VMEM((2, 2, 3, ROWS, 3 * S), bf16),
            pltpu.VMEM((4, 2, ROWS, WIDE[0]), f32),
            pltpu.VMEM((2, 2, 2, ROWS, WIDE[1]), f32),
            pltpu.VMEM((2, 3, ROWS, S), f32),
            pltpu.VMEM((4, 2, ROWS, WIDE[0]), f32),
            pltpu.VMEM((2, 2, ROWS, WIDE[1]), f32),
        ]
        + [pltpu.VMEM(shape, f32) for shape in sends]
        + [pltpu.VMEM(shape, f32) for shape in turns]
        + [
            pltpu.SemaphoreType.DMA((2 + CHUNKS, ROLES)),
            pltpu.SemaphoreType.DMA((2 + CHUNKS, ROLES)),
            pltpu.SemaphoreType.DMA((4, 4)),
            pltpu.SemaphoreType.DMA((4, 4)),
            pltpu.SemaphoreType.DMA((3, PROCS)),
            pltpu.SemaphoreType.DMA((3, PROCS)),
        ],
        compiler_params=pltpu.CompilerParams(
            collective_id=0, has_side_effects=True, vmem_limit_bytes=62 * 2**20
        ),
    )(*arguments)


def solution(mesh):
    in_specs = (
        P(),
        P(None, "proc", None),
        P(None, "proc", "group"),
        P(None, "proc", "group"),
        P(None, "proc", "group"),
        P(None, None, "proc", "group"),
        P(None, None, "proc", "group"),
        P(None, None, "proc", "group"),
    )
    out_specs = (
        P(None, None, "proc", "group"),
        P(None, None, "proc", "group"),
        P(None, None, "proc", "group"),
        P(None, "proc", "group"),
        P(None, "proc", "group"),
        P(None, "proc", "group"),
    )
    return jax.shard_map(shards, mesh=mesh, in_specs=in_specs, out_specs=out_specs, check_vma=False)
```

```python
import jax
import jax.numpy as jnp
from jax import lax
from jax.experimental import pallas as pl
from jax.experimental.pallas import tpu as pltpu
from jax.sharding import PartitionSpec as P

MESH = pl.DeviceIdType.MESH
S = 768
PROCS = 16
ROWS = S // PROCS
HALF = ROWS // 2
CHUNKS = 3
WIDTH = S // CHUNKS
WIDE = (256, 384)
COLS = (192, 384)
ROLES = 17
X_FIRST = ((2, 1), (3, 1), (4, 1))


def split(value):
    high = value.astype(jnp.bfloat16)
    low = (value - high.astype(jnp.float32)).astype(jnp.bfloat16)
    return high, low


def dot(first, second):
    return jnp.dot(first, second, preferred_element_type=jnp.float32)


def complex_rows(high, low, real_high, real_low, imag_high, imag_low):
    both = high.shape[0]
    half = both // 2
    stacked = jnp.concatenate([high, low], axis=0)
    by_real = dot(stacked, real_high)
    by_real = by_real[:both] + by_real[both:] + dot(high, real_low)
    by_imag = dot(stacked, imag_high)
    by_imag = by_imag[:both] + by_imag[both:] + dot(high, imag_low)
    return by_real[:half] - by_imag[half:], by_imag[:half] + by_real[half:]


def kernel(
    pattern,
    inverse_root,
    inverse_one,
    inverse_two,
    inverse_three,
    lower_one,
    lower_two,
    lower_three,
    upper_one,
    upper_two,
    upper_three,
    diagonal_one,
    diagonal_two,
    diagonal_three,
    full_one,
    full_two,
    full_three,
    high_one,
    high_two,
    high_three,
    low_one,
    low_two,
    low_three,
    chain,
    join_one,
    join_two,
    joined,
    join_diag_one,
    join_diag_two,
    send_one,
    send_two,
    send_three,
    turned_one,
    turned_two,
    turned_three,
    gather_send,
    gather_recv,
    join_send,
    join_recv,
    turn_send,
    turn_recv,
):
    group = lax.axis_index("group")
    me = lax.axis_index("proc")
    x_at = me // 4
    y_at = me // 2 % 2
    core = me % 2

    def proc_of(dx, dy, dc=0):
        return lax.rem(x_at + dx, 4) * 4 + lax.rem(y_at + dy, 2) * 2 + lax.rem(core + dc, 2)

    right, left = proc_of(1, 0), proc_of(3, 0)
    far, pair, sibling = proc_of(2, 0), proc_of(0, 1), proc_of(0, 0, 1)
    pair_right, pair_left, pair_far = proc_of(1, 1), proc_of(3, 1), proc_of(2, 1)

    barrier = pltpu.get_barrier_semaphore()
    for step in range(1, PROCS):
        pl.semaphore_signal(
            barrier, inc=1, device_id=(group, lax.rem(me + step, PROCS)), device_id_type=MESH
        )
    for flip in range(1, 4):
        pl.semaphore_signal(barrier, inc=1, device_id=(group ^ flip, me), device_id_type=MESH)

    def keep(level, a):
        node = group // 2 ** (3 - level)
        first = (level - 2) * 2**level + 2
        return pattern[first + node * level + a].astype(jnp.float32)

    buffers = [full_one, full_two] + [full_three.at[c] for c in range(CHUNKS)]
    highs = [high_one, high_two] + [high_three.at[c] for c in range(CHUNKS)]
    lows = [low_one, low_two] + [low_three.at[c] for c in range(CHUNKS)]

    def rows_of(proc, offset=0):
        return pl.multiple_of(proc * ROWS + offset, 8)

    own = pl.ds(rows_of(me), ROWS)
    full_one[:, :, own, :] = jnp.zeros((2, 1, ROWS, WIDE[0]), jnp.float32)
    full_one[:, 0, own, : COLS[0]] = lower_one[:, 0] * keep(1, 0)
    for a in range(2):
        full_two[:, a, own, :] = lower_two[:, a] * keep(2, a)
    for a in range(3):
        for c in range(CHUNKS):
            full_three[c, :, a, own, :] = (
                lower_three[:, a, :, c * WIDTH : (c + 1) * WIDTH] * keep(3, a)
            )
    for part in range(2):
        high, low = split(inverse_root[part])
        chain[0, part, 0, :, :S] = high
        chain[1, part, 0, :, :S] = low

    pl.semaphore_wait(barrier, PROCS - 1 + 3)

    pending = []

    def block(chunk, part, proc, half):
        offset, count = (0, ROWS) if half is None else (half * HALF, HALF)
        return buffers[chunk].at[part, :, pl.ds(rows_of(proc, offset), count), :]

    def gather_copy(chunk, part, role, proc, to, half):
        place = block(chunk, part, proc, half)
        return pltpu.make_async_remote_copy(
            src_ref=place,
            dst_ref=place,
            send_sem=gather_send.at[chunk, part, role],
            recv_sem=gather_recv.at[chunk, part, role],
            device_id=(group, to),
            device_id_type=MESH,
        )

    def send(chunk, part, role, proc, to, half=None):
        copy = gather_copy(chunk, part, role, proc, to, half)
        copy.start()
        pending.append(copy)

    def arrive(chunk, part, role, proc, half=None):
        gather_copy(chunk, part, role, proc, sibling, half).wait_recv()

    def x_first(q, part):
        return (q, part) in X_FIRST

    def stage_a(q):
        for part in range(2):
            send(q, part, 0, me, pair)
        for part in range(2):
            send(q, part, 1, me, right)
            send(q, part, 2, me, left)
        for part in range(2):
            send(q, part, 9, me, sibling)

    def stage_b(q):
        for part in range(2):
            if not x_first(q, part):
                arrive(q, part, 0, pair)
                send(q, part, 3, pair, right)
                send(q, part, 4, pair, left)
                send(q, part, 10, pair, sibling)
        for part in range(2):
            arrive(q, part, 1, left)
            send(q, part, 5, left, right, 0)
            if x_first(q, part):
                send(q, part, 3, left, pair)
            send(q, part, 11, left, sibling)
            arrive(q, part, 2, right)
            send(q, part, 6, right, left, 1)
            if x_first(q, part):
                send(q, part, 4, right, pair)
            send(q, part, 12, right, sibling)

    def stage_c(q):
        for part in range(2):
            arrive(q, part, 5, far, 0)
            arrive(q, part, 6, far, 1)
            if x_first(q, part):
                send(q, part, 7, far, pair)
                arrive(q, part, 0, pair)
                send(q, part, 10, pair, sibling)
            send(q, part, 15, far, sibling)
        for part in range(2):
            if not x_first(q, part):
                arrive(q, part, 3, pair_left)
                send(q, part, 7, pair_left, right, 0)
                send(q, part, 13, pair_left, sibling)
                arrive(q, part, 4, pair_right)
                send(q, part, 8, pair_right, left, 1)
                send(q, part, 14, pair_right, sibling)

    def stage_d(q):
        for part in range(2):
            if x_first(q, part):
                arrive(q, part, 3, pair_left)
                send(q, part, 13, pair_left, sibling)
                arrive(q, part, 4, pair_right)
                send(q, part, 14, pair_right, sibling)
                arrive(q, part, 7, pair_far)
            else:
                arrive(q, part, 7, pair_far, 0)
                arrive(q, part, 8, pair_far, 1)
            send(q, part, 16, pair_far, sibling)

    def stage_e(q):
        flip = 1 - 2 * core
        sources = (me, pair, left, right, pair_left, pair_right, far, pair_far)
        for part in range(2):
            for at, proc in enumerate(sources):
                arrive(q, part, 9 + at, proc + flip)

    def convert(q):
        for part in range(2):
            for a in range(buffers[q].shape[1]):
                high, low = split(buffers[q][part, a])
                highs[q][part, a] = high
                lows[q][part, a] = low

    def factors(q):
        levels, width = highs[q].shape[1], highs[q].shape[3]
        return [
            ref[part].reshape(levels * S, width) for part in range(2) for ref in (highs[q], lows[q])
        ]

    def new_upper(q, level):
        depth = level * S
        rows = 2 * level * ROWS
        high = chain[0, :, :level, :, :depth].reshape(rows, depth)
        low = chain[1, :, :level, :, :depth].reshape(rows, depth)
        real, imag = complex_rows(high, low, *factors(q))
        shape = (level, ROWS, highs[q].shape[3])
        return -real.reshape(shape), -imag.reshape(shape)

    def join_copies(step, flips, ref, slot):
        copies = []
        for flip in flips:
            copy = pltpu.make_async_remote_copy(
                src_ref=ref.at[slot],
                dst_ref=ref.at[slot],
                send_sem=join_send.at[step, flip],
                recv_sem=join_recv.at[step, flip],
                device_id=(group ^ flip, me),
                device_id_type=MESH,
            )
            copy.start()
            copies.append(copy)
        pending.extend(copies)

    def join_waits(step, flips, ref, slot):
        for flip in flips:
            place = ref.at[slot ^ flip]
            pltpu.make_async_remote_copy(
                src_ref=place,
                dst_ref=place,
                send_sem=join_send.at[step, flip],
                recv_sem=join_recv.at[step, flip],
                device_id=(group ^ flip, me),
                device_id_type=MESH,
            ).wait_recv()

    def widen(pieces):
        lane = lax.broadcasted_iota(jnp.int32, (pieces[0].shape[0], 128), 1)
        tiles = []
        for even, odd in ((pieces[0], pieces[1]), (pieces[2], pieces[3])):
            rolled = pltpu.roll(odd, 64, 1)
            tiles += [
                even[:, :128],
                jnp.where(lane < 64, even[:, 128:], rolled[:, :128]),
                rolled[:, 128:],
            ]
        return jnp.concatenate(tiles, axis=1)

    def window(real, imag, proc, base=0):
        start = proc * ROWS - base
        tile, shift = start // 128 * 128, start % 128
        count = 128 if shift + ROWS <= 128 else 256
        lane = lax.broadcasted_iota(jnp.int32, (real.shape[0], 128), 1)
        first = real[:, tile : tile + count]
        second = imag[:, tile : tile + count]
        if shift:
            first = pltpu.roll(first, count - shift, 1)[:, :128]
        if shift != ROWS:
            second = pltpu.roll(second, (count + ROWS - shift) % count, 1)[:, :128]
        return jnp.where(lane < ROWS, first[:, :128], second[:, :128])

    def turn_copy(level, source, target, to):
        return pltpu.make_async_remote_copy(
            src_ref=source.at[to],
            dst_ref=target.at[:, own, :],
            send_sem=turn_send.at[level - 1, to],
            recv_sem=turn_recv.at[level - 1, me],
            device_id=(group, to),
            device_id_type=MESH,
        )

    def turn_arrive(level, source, target, proc):
        pltpu.make_async_remote_copy(
            src_ref=source.at[proc],
            dst_ref=target.at[:, pl.ds(rows_of(proc), ROWS), :],
            send_sem=turn_send.at[level - 1, proc],
            recv_sem=turn_recv.at[level - 1, proc],
            device_id=(group, proc),
            device_id_type=MESH,
        ).wait_recv()

    def turn_start(level, source, target):
        real = joined[0, :level].reshape(level * ROWS, S)
        imag = joined[1, :level].reshape(level * ROWS, S)
        for proc in range(PROCS):
            source[proc] = window(real, imag, proc).reshape(level, ROWS, 128)
        for step in range(1, PROCS):
            copy = turn_copy(level, source, target, lax.rem(me + step, PROCS))
            copy.start()
            pending.append(copy)
        target[:, own, :] = source[me]

    def turn_finish(level, source, target):
        for step in range(1, PROCS):
            turn_arrive(level, source, target, lax.rem(me + PROCS - step, PROCS))
        flat = target[...].reshape(level * S, 128)
        return split(flat.T[: 2 * ROWS])

    def new_diagonal(q, row_high, row_low):
        return complex_rows(row_high, row_low, *factors(q))

    def put_chain(part, a, columns, value):
        high, low = split(value)
        chain[0, part, a, :, columns] = high
        chain[1, part, a, :, columns] = low

    slot_one, slot_two = lax.rem(group, 4), lax.rem(group, 2)
    flips_one, flips_two = (1, 2, 3), (1,)

    stage_a(0)
    stage_a(1)
    stage_b(0)
    stage_a(2)
    stage_c(0)
    stage_b(1)
    stage_d(0)
    stage_e(0)
    convert(0)
    real, imag = new_upper(0, 1)
    for part, value in ((0, real), (1, imag)):
        upper_one[part] = value[:, :, : COLS[0]]
        join_one[slot_one, part] = value[0]
    join_copies(0, flips_one, join_one, slot_one)
    stage_a(3)
    stage_c(1)
    stage_b(2)
    join_waits(0, flips_one, join_one, slot_one)
    for part in range(2):
        value = widen([join_one[j, part] for j in range(4)])
        joined[part, 0] = value
        put_chain(part, 0, slice(S, 2 * S), value)
    turn_start(1, send_one, turned_one)
    stage_d(1)
    stage_a(4)
    row_high, row_low = turn_finish(1, send_one, turned_one)
    for part in range(2):
        rows = slice(part * ROWS, (part + 1) * ROWS)
        chain[0, part, 1, :, :S] = row_high[rows]
        chain[1, part, 1, :, :S] = row_low[rows]
    product = new_diagonal(0, row_high, row_low)
    for part in range(2):
        value = inverse_one[part] - product[part][:, : COLS[0]]
        diagonal_one[part] = value
        join_diag_one[slot_one, part, :, : COLS[0]] = value
    join_copies(1, flips_one, join_diag_one, slot_one)
    stage_c(2)
    stage_b(3)
    stage_e(1)
    join_waits(1, flips_one, join_diag_one, slot_one)
    for part in range(2):
        value = widen([join_diag_one[j, part] for j in range(4)])
        put_chain(part, 1, slice(S, 2 * S), value)

    convert(1)
    real, imag = new_upper(1, 2)
    for part, value in ((0, real), (1, imag)):
        upper_two[part] = value
        join_two[slot_two, part] = value
    join_copies(2, flips_two, join_two, slot_two)
    stage_d(2)
    stage_c(3)
    join_waits(2, flips_two, join_two, slot_two)
    for part in range(2):
        for j in range(2):
            columns = slice(j * COLS[1], (j + 1) * COLS[1])
            for a in range(2):
                value = join_two[j, part, a]
                joined[part, a, :, columns] = value
                put_chain(part, a, slice(2 * S + j * COLS[1], 2 * S + (j + 1) * COLS[1]), value)
    turn_start(2, send_two, turned_two)
    stage_b(4)
    stage_e(2)
    row_high, row_low = turn_finish(2, send_two, turned_two)
    for part in range(2):
        rows = slice(part * ROWS, (part + 1) * ROWS)
        chain[0, part, 2, :, : 2 * S] = row_high[rows]
        chain[1, part, 2, :, : 2 * S] = row_low[rows]
    product = new_diagonal(1, row_high, row_low)
    for part in range(2):
        value = inverse_two[part] - product[part]
        diagonal_two[part] = value
        join_diag_two[slot_two, part] = value
    join_copies(3, flips_two, join_diag_two, slot_two)
    stage_d(3)
    stage_c(4)
    join_waits(3, flips_two, join_diag_two, slot_two)
    for part in range(2):
        for j in range(2):
            put_chain(
                part,
                2,
                slice(2 * S + j * COLS[1], 2 * S + (j + 1) * COLS[1]),
                join_diag_two[j, part],
            )

    done = 0
    for c in range(CHUNKS):
        q = 2 + c
        if c == 1:
            stage_e(3)
        if c == 2:
            stage_d(4)
            stage_e(4)
        convert(q)
        real, imag = new_upper(q, 3)
        columns = slice(c * WIDTH, (c + 1) * WIDTH)
        for part, value in ((0, real), (1, imag)):
            upper_three[part, :, :, columns] = value
            joined[part, :, :, columns] = value
        ready = (c + 1) * WIDTH // ROWS
        for proc in range(done, ready):
            real = joined[0].reshape(3 * ROWS, S)
            imag = joined[1].reshape(3 * ROWS, S)
            send_three[proc] = window(real, imag, proc).reshape(3, ROWS, 128)

            @pl.when(me != proc)
            def _():
                turn_copy(3, send_three, turned_three, proc).start()

        done = ready
    turned_three[:, own, :] = send_three[me]
    row_high, row_low = turn_finish(3, send_three, turned_three)
    for c in range(CHUNKS):
        columns = slice(c * WIDTH, (c + 1) * WIDTH)
        product = new_diagonal(2 + c, row_high, row_low)
        for part in range(2):
            diagonal_three[part, :, columns] = inverse_three[part, :, columns] - product[part]

    for copy in pending:
        copy.wait_send()
    for step in range(1, PROCS):
        turn_copy(3, send_three, turned_three, lax.rem(me + step, PROCS)).wait_send()


def hand_over(*refs):
    for at in range(6):
        refs[at + 6][...] = refs[at][...]


def shards(*arguments):
    f32, bf16 = jnp.float32, jnp.bfloat16
    outputs = [jax.ShapeDtypeStruct(a.shape, f32) for a in arguments[5:8] + arguments[2:5]]
    vmem = pl.BlockSpec(memory_space=pltpu.VMEM)
    fulls = [(2, 1, S, WIDE[0]), (2, 2, S, WIDE[1]), (CHUNKS, 2, 3, S, WIDTH)]
    sends = [(PROCS, level, ROWS, 128) for level in (1, 2, 3)]
    turns = [(level, S, 128) for level in (1, 2, 3)]
    results = pl.pallas_call(
        kernel,
        out_shape=outputs,
        in_specs=[pl.BlockSpec(memory_space=pltpu.SMEM)] + [vmem] * 7,
        out_specs=[vmem] * 6,
        scratch_shapes=[pltpu.VMEM(shape, f32) for shape in fulls]
        + [pltpu.VMEM(shape, bf16) for shape in fulls]
        + [pltpu.VMEM(shape, bf16) for shape in fulls]
        + [
            pltpu.VMEM((2, 2, 3, ROWS, 3 * S), bf16),
            pltpu.VMEM((4, 2, ROWS, WIDE[0]), f32),
            pltpu.VMEM((2, 2, 2, ROWS, WIDE[1]), f32),
            pltpu.VMEM((2, 3, ROWS, S), f32),
            pltpu.VMEM((4, 2, ROWS, WIDE[0]), f32),
            pltpu.VMEM((2, 2, ROWS, WIDE[1]), f32),
        ]
        + [pltpu.VMEM(shape, f32) for shape in sends]
        + [pltpu.VMEM(shape, f32) for shape in turns]
        + [
            pltpu.SemaphoreType.DMA((2 + CHUNKS, 2, ROLES)),
            pltpu.SemaphoreType.DMA((2 + CHUNKS, 2, ROLES)),
            pltpu.SemaphoreType.DMA((4, 4)),
            pltpu.SemaphoreType.DMA((4, 4)),
            pltpu.SemaphoreType.DMA((3, PROCS)),
            pltpu.SemaphoreType.DMA((3, PROCS)),
        ],
        compiler_params=pltpu.CompilerParams(
            collective_id=0, has_side_effects=True, vmem_limit_bytes=62 * 2**20
        ),
    )(*arguments)
    return pl.pallas_call(
        hand_over,
        out_shape=outputs,
        in_specs=[vmem] * 6,
        out_specs=[vmem] * 6,
    )(*results)


def solution(mesh):
    in_specs = (
        P(),
        P(None, "proc", None),
        P(None, "proc", "group"),
        P(None, "proc", "group"),
        P(None, "proc", "group"),
        P(None, None, "proc", "group"),
        P(None, None, "proc", "group"),
        P(None, None, "proc", "group"),
    )
    out_specs = (
        P(None, None, "proc", "group"),
        P(None, None, "proc", "group"),
        P(None, None, "proc", "group"),
        P(None, "proc", "group"),
        P(None, "proc", "group"),
        P(None, "proc", "group"),
    )
    return jax.shard_map(shards, mesh=mesh, in_specs=in_specs, out_specs=out_specs, check_vma=False)
```

```python
import jax
import jax.numpy as jnp
from jax import lax
from jax.experimental import pallas as pl
from jax.experimental.pallas import tpu as pltpu
from jax.sharding import PartitionSpec as P

MESH = pl.DeviceIdType.MESH
S = 768
PROCS = 16
ROWS = S // PROCS
HALF = ROWS // 2
CHUNKS = 3
WIDTH = S // CHUNKS
WIDE = (256, 384)
COLS = (192, 384)
ROLES = 17
X_FIRST = ((2, 1), (3, 1))


def split(value):
    high = value.astype(jnp.bfloat16)
    low = (value - high.astype(jnp.float32)).astype(jnp.bfloat16)
    return high, low


def dot(first, second):
    return jnp.dot(first, second, preferred_element_type=jnp.float32)


def complex_rows(high, low, real_high, real_low, imag_high, imag_low):
    both = high.shape[0]
    half = both // 2
    stacked = jnp.concatenate([high, low], axis=0)
    by_real = dot(stacked, real_high)
    by_real = by_real[:both] + by_real[both:] + dot(high, real_low)
    by_imag = dot(stacked, imag_high)
    by_imag = by_imag[:both] + by_imag[both:] + dot(high, imag_low)
    return by_real[:half] - by_imag[half:], by_imag[:half] + by_real[half:]


def kernel(
    pattern,
    inverse_root,
    inverse_one,
    inverse_two,
    inverse_three,
    lower_one,
    lower_two,
    lower_three,
    upper_one,
    upper_two,
    upper_three,
    diagonal_one,
    diagonal_two,
    diagonal_three,
    full_one,
    full_two,
    full_three,
    high_one,
    high_two,
    high_three,
    low_one,
    low_two,
    low_three,
    chain,
    join_one,
    join_two,
    joined,
    join_diag_one,
    join_diag_two,
    send_one,
    send_two,
    send_three,
    turned_one,
    turned_two,
    turned_three,
    gather_send,
    gather_recv,
    join_send,
    join_recv,
    turn_send,
    turn_recv,
):
    group = lax.axis_index("group")
    me = lax.axis_index("proc")
    x_at = me // 4
    y_at = me // 2 % 2
    core = me % 2

    def proc_of(dx, dy, dc=0):
        return lax.rem(x_at + dx, 4) * 4 + lax.rem(y_at + dy, 2) * 2 + lax.rem(core + dc, 2)

    right, left = proc_of(1, 0), proc_of(3, 0)
    far, pair, sibling = proc_of(2, 0), proc_of(0, 1), proc_of(0, 0, 1)
    pair_right, pair_left, pair_far = proc_of(1, 1), proc_of(3, 1), proc_of(2, 1)

    barrier = pltpu.get_barrier_semaphore()
    for step in range(1, PROCS):
        pl.semaphore_signal(
            barrier, inc=1, device_id=(group, lax.rem(me + step, PROCS)), device_id_type=MESH
        )
    for flip in range(1, 4):
        pl.semaphore_signal(barrier, inc=1, device_id=(group ^ flip, me), device_id_type=MESH)

    def keep(level, a):
        node = group // 2 ** (3 - level)
        first = (level - 2) * 2**level + 2
        return pattern[first + node * level + a].astype(jnp.float32)

    buffers = [full_one, full_two] + [full_three.at[c] for c in range(CHUNKS)]
    highs = [high_one, high_two] + [high_three.at[c] for c in range(CHUNKS)]
    lows = [low_one, low_two] + [low_three.at[c] for c in range(CHUNKS)]

    def rows_of(proc, offset=0):
        return pl.multiple_of(proc * ROWS + offset, 8)

    own = pl.ds(rows_of(me), ROWS)
    full_one[:, :, own, :] = jnp.zeros((2, 1, ROWS, WIDE[0]), jnp.float32)
    full_one[:, 0, own, : COLS[0]] = lower_one[:, 0] * keep(1, 0)
    for a in range(2):
        full_two[:, a, own, :] = lower_two[:, a] * keep(2, a)
    for a in range(3):
        for c in range(CHUNKS):
            full_three[c, :, a, own, :] = (
                lower_three[:, a, :, c * WIDTH : (c + 1) * WIDTH] * keep(3, a)
            )
    for part in range(2):
        high, low = split(inverse_root[part])
        chain[0, part, 0, :, :S] = high
        chain[1, part, 0, :, :S] = low

    pl.semaphore_wait(barrier, PROCS - 1 + 3)

    pending = []

    def block(chunk, part, proc, half):
        offset, count = (0, ROWS) if half is None else (half * HALF, HALF)
        return buffers[chunk].at[part, :, pl.ds(rows_of(proc, offset), count), :]

    def gather_copy(chunk, part, role, proc, to, half):
        place = block(chunk, part, proc, half)
        return pltpu.make_async_remote_copy(
            src_ref=place,
            dst_ref=place,
            send_sem=gather_send.at[chunk, part, role],
            recv_sem=gather_recv.at[chunk, part, role],
            device_id=(group, to),
            device_id_type=MESH,
        )

    def send(chunk, part, role, proc, to, half=None):
        copy = gather_copy(chunk, part, role, proc, to, half)
        copy.start()
        pending.append(copy)

    def arrive(chunk, part, role, proc, half=None):
        gather_copy(chunk, part, role, proc, sibling, half).wait_recv()

    def x_first(q, part):
        return (q, part) in X_FIRST

    def stage_a(q):
        for part in range(2):
            send(q, part, 0, me, pair)
        for part in range(2):
            send(q, part, 1, me, right)
            send(q, part, 2, me, left)
        for part in range(2):
            send(q, part, 9, me, sibling)

    def stage_b(q):
        for part in range(2):
            if not x_first(q, part):
                arrive(q, part, 0, pair)
                send(q, part, 3, pair, right)
                send(q, part, 4, pair, left)
                send(q, part, 10, pair, sibling)
        for part in range(2):
            arrive(q, part, 1, left)
            send(q, part, 5, left, right, 0)
            if x_first(q, part):
                send(q, part, 3, left, pair)
            send(q, part, 11, left, sibling)
            arrive(q, part, 2, right)
            send(q, part, 6, right, left, 1)
            if x_first(q, part):
                send(q, part, 4, right, pair)
            send(q, part, 12, right, sibling)

    def stage_c(q):
        for part in range(2):
            arrive(q, part, 5, far, 0)
            arrive(q, part, 6, far, 1)
            if x_first(q, part):
                send(q, part, 7, far, pair)
                arrive(q, part, 0, pair)
                send(q, part, 10, pair, sibling)
            send(q, part, 15, far, sibling)
        for part in range(2):
            if not x_first(q, part):
                arrive(q, part, 3, pair_left)
                send(q, part, 7, pair_left, right, 0)
                send(q, part, 13, pair_left, sibling)
                arrive(q, part, 4, pair_right)
                send(q, part, 8, pair_right, left, 1)
                send(q, part, 14, pair_right, sibling)

    def stage_d(q):
        for part in range(2):
            if x_first(q, part):
                arrive(q, part, 3, pair_left)
                send(q, part, 13, pair_left, sibling)
                arrive(q, part, 4, pair_right)
                send(q, part, 14, pair_right, sibling)
                arrive(q, part, 7, pair_far)
            else:
                arrive(q, part, 7, pair_far, 0)
                arrive(q, part, 8, pair_far, 1)
            send(q, part, 16, pair_far, sibling)

    def stage_e(q):
        flip = 1 - 2 * core
        sources = (me, pair, left, right, pair_left, pair_right, far, pair_far)
        for part in range(2):
            for at, proc in enumerate(sources):
                arrive(q, part, 9 + at, proc + flip)

    def convert(q):
        for part in range(2):
            for a in range(buffers[q].shape[1]):
                high, low = split(buffers[q][part, a])
                highs[q][part, a] = high
                lows[q][part, a] = low

    def factors(q):
        levels, width = highs[q].shape[1], highs[q].shape[3]
        return [
            ref[part].reshape(levels * S, width) for part in range(2) for ref in (highs[q], lows[q])
        ]

    def new_upper(q, level, first, last):
        depth = level * S
        rows = 2 * (last - first) * ROWS
        high = chain[0, :, first:last, :, :depth].reshape(rows, depth)
        low = chain[1, :, first:last, :, :depth].reshape(rows, depth)
        real, imag = complex_rows(high, low, *factors(q))
        shape = (last - first, ROWS, highs[q].shape[3])
        return -real.reshape(shape), -imag.reshape(shape)

    def join_copies(step, flips, ref, slot, at=()):
        copies = []
        for flip in flips:
            copy = pltpu.make_async_remote_copy(
                src_ref=ref.at[(slot, *at)],
                dst_ref=ref.at[(slot, *at)],
                send_sem=join_send.at[step, flip],
                recv_sem=join_recv.at[step, flip],
                device_id=(group ^ flip, me),
                device_id_type=MESH,
            )
            copy.start()
            copies.append(copy)
        pending.extend(copies)

    def join_waits(step, flips, ref, slot, at=()):
        for flip in flips:
            place = ref.at[(slot ^ flip, *at)]
            pltpu.make_async_remote_copy(
                src_ref=place,
                dst_ref=place,
                send_sem=join_send.at[step, flip],
                recv_sem=join_recv.at[step, flip],
                device_id=(group ^ flip, me),
                device_id_type=MESH,
            ).wait_recv()

    def widen(pieces):
        lane = lax.broadcasted_iota(jnp.int32, (pieces[0].shape[0], 128), 1)
        tiles = []
        for even, odd in ((pieces[0], pieces[1]), (pieces[2], pieces[3])):
            rolled = pltpu.roll(odd, 64, 1)
            tiles += [
                even[:, :128],
                jnp.where(lane < 64, even[:, 128:], rolled[:, :128]),
                rolled[:, 128:],
            ]
        return jnp.concatenate(tiles, axis=1)

    def window(real, imag, proc, base=0):
        start = proc * ROWS - base
        tile, shift = start // 128 * 128, start % 128
        count = 128 if shift + ROWS <= 128 else 256
        lane = lax.broadcasted_iota(jnp.int32, (real.shape[0], 128), 1)
        first = real[:, tile : tile + count]
        second = imag[:, tile : tile + count]
        if shift:
            first = pltpu.roll(first, count - shift, 1)[:, :128]
        if shift != ROWS:
            second = pltpu.roll(second, (count + ROWS - shift) % count, 1)[:, :128]
        return jnp.where(lane < ROWS, first[:, :128], second[:, :128])

    def turn_copy(turn, source, target, span, to):
        return pltpu.make_async_remote_copy(
            src_ref=source.at[to, span],
            dst_ref=target.at[span, own, :],
            send_sem=turn_send.at[turn, to],
            recv_sem=turn_recv.at[turn, me],
            device_id=(group, to),
            device_id_type=MESH,
        )

    def turn_arrive(turn, source, target, span, proc):
        pltpu.make_async_remote_copy(
            src_ref=source.at[proc, span],
            dst_ref=target.at[span, pl.ds(rows_of(proc), ROWS), :],
            send_sem=turn_send.at[turn, proc],
            recv_sem=turn_recv.at[turn, proc],
            device_id=(group, proc),
            device_id_type=MESH,
        ).wait_recv()

    def fill(source, first, last, proc):
        rows = (last - first) * ROWS
        real = joined[0, first:last].reshape(rows, S)
        imag = joined[1, first:last].reshape(rows, S)
        source[proc, first:last] = window(real, imag, proc).reshape(last - first, ROWS, 128)

    def turn_start(turn, source, target, first, last):
        span = slice(first, last)
        for proc in range(PROCS):
            fill(source, first, last, proc)
        for step in range(1, PROCS):
            copy = turn_copy(turn, source, target, span, lax.rem(me + step, PROCS))
            copy.start()
            pending.append(copy)
        target[span, own, :] = source[me, span]

    def turn_wait(turn, source, target, first, last):
        for step in range(1, PROCS):
            proc = lax.rem(me + PROCS - step, PROCS)
            turn_arrive(turn, source, target, slice(first, last), proc)

    def turned_rows(target):
        flat = target[...].reshape(target.shape[0] * S, 128)
        return split(flat.T[: 2 * ROWS])

    def new_diagonal(q, row_high, row_low):
        return complex_rows(row_high, row_low, *factors(q))

    def put_chain(part, a, columns, value):
        high, low = split(value)
        chain[0, part, a, :, columns] = high
        chain[1, part, a, :, columns] = low

    slot_one, slot_two = lax.rem(group, 4), lax.rem(group, 2)
    flips_one, flips_two = (1, 2, 3), (1,)

    stage_a(0)
    stage_a(1)
    stage_b(0)
    stage_a(2)
    stage_c(0)
    stage_b(1)
    stage_d(0)
    stage_e(0)
    convert(0)
    real, imag = new_upper(0, 1, 0, 1)
    for part, value in ((0, real), (1, imag)):
        upper_one[part] = value[:, :, : COLS[0]]
        join_one[slot_one, part] = value[0]
    join_copies(0, flips_one, join_one, slot_one)
    stage_a(3)
    stage_c(1)
    stage_b(2)
    join_waits(0, flips_one, join_one, slot_one)
    for part in range(2):
        value = widen([join_one[j, part] for j in range(4)])
        joined[part, 0] = value
        put_chain(part, 0, slice(S, 2 * S), value)
    turn_start(0, send_one, turned_one, 0, 1)
    stage_d(1)
    stage_a(4)
    turn_wait(0, send_one, turned_one, 0, 1)
    row_high, row_low = turned_rows(turned_one)
    for part in range(2):
        rows = slice(part * ROWS, (part + 1) * ROWS)
        chain[0, part, 1, :, :S] = row_high[rows]
        chain[1, part, 1, :, :S] = row_low[rows]
    product = new_diagonal(0, row_high, row_low)
    for part in range(2):
        value = inverse_one[part] - product[part][:, : COLS[0]]
        diagonal_one[part] = value
        join_diag_one[slot_one, part, :, : COLS[0]] = value
    join_copies(1, flips_one, join_diag_one, slot_one)
    stage_c(2)
    stage_b(3)
    stage_e(1)

    convert(1)

    def upper_two_rows(a):
        real, imag = new_upper(1, 2, a, a + 1)
        for part, value in ((0, real), (1, imag)):
            upper_two[part, a] = value[0]
            join_two[slot_two, part, a] = value[0]
        join_copies(2 + a, flips_two, join_two, slot_two, (slice(None), a))

    def join_two_rows(a):
        join_waits(2 + a, flips_two, join_two, slot_two, (slice(None), a))
        for part in range(2):
            for j in range(2):
                value = join_two[j, part, a]
                joined[part, a, :, j * COLS[1] : (j + 1) * COLS[1]] = value
                put_chain(part, a, slice(2 * S + j * COLS[1], 2 * S + (j + 1) * COLS[1]), value)
        turn_start(1 + a, send_two, turned_two, a, a + 1)

    upper_two_rows(0)
    join_waits(1, flips_one, join_diag_one, slot_one)
    for part in range(2):
        value = widen([join_diag_one[j, part] for j in range(4)])
        put_chain(part, 1, slice(S, 2 * S), value)
    upper_two_rows(1)
    join_two_rows(0)
    stage_d(2)
    stage_c(3)
    join_two_rows(1)
    stage_b(4)
    stage_e(2)

    def upper_three_rows(c, first, last):
        real, imag = new_upper(2 + c, 3, first, last)
        columns = slice(c * WIDTH, (c + 1) * WIDTH)
        for part, value in ((0, real), (1, imag)):
            upper_three[part, first:last, :, columns] = value
            joined[part, first:last, :, columns] = value

    def turn_three(c):
        for proc in range(c * WIDTH // ROWS, (c + 1) * WIDTH // ROWS):
            fill(send_three, 0, 3, proc)

            @pl.when(me != proc)
            def _():
                turn_copy(3, send_three, turned_three, slice(0, 3), proc).start()

    convert(2)
    upper_three_rows(0, 0, 2)
    for a in range(2):
        turn_wait(1 + a, send_two, turned_two, a, a + 1)
    row_high, row_low = turned_rows(turned_two)
    for part in range(2):
        rows = slice(part * ROWS, (part + 1) * ROWS)
        chain[0, part, 2, :, : 2 * S] = row_high[rows]
        chain[1, part, 2, :, : 2 * S] = row_low[rows]
    product = new_diagonal(1, row_high, row_low)
    for part in range(2):
        value = inverse_two[part] - product[part]
        diagonal_two[part] = value
        join_diag_two[slot_two, part] = value
    join_copies(4, flips_two, join_diag_two, slot_two)
    stage_d(3)
    stage_c(4)
    stage_e(3)
    convert(3)
    upper_three_rows(1, 0, 2)
    join_waits(4, flips_two, join_diag_two, slot_two)
    for part in range(2):
        for j in range(2):
            put_chain(
                part,
                2,
                slice(2 * S + j * COLS[1], 2 * S + (j + 1) * COLS[1]),
                join_diag_two[j, part],
            )
    upper_three_rows(0, 2, 3)
    turn_three(0)
    stage_d(4)
    upper_three_rows(1, 2, 3)
    turn_three(1)
    stage_e(4)
    convert(4)
    upper_three_rows(2, 0, 3)
    turn_three(2)
    turned_three[:, own, :] = send_three[me]
    turn_wait(3, send_three, turned_three, 0, 3)
    row_high, row_low = turned_rows(turned_three)
    for c in range(CHUNKS):
        columns = slice(c * WIDTH, (c + 1) * WIDTH)
        product = new_diagonal(2 + c, row_high, row_low)
        for part in range(2):
            diagonal_three[part, :, columns] = inverse_three[part, :, columns] - product[part]

    for copy in pending:
        copy.wait_send()
    for step in range(1, PROCS):
        to = lax.rem(me + step, PROCS)
        turn_copy(3, send_three, turned_three, slice(0, 3), to).wait_send()


def hand_over(*refs):
    for at in range(6):
        refs[at + 6][...] = refs[at][...]


def shards(*arguments):
    f32, bf16 = jnp.float32, jnp.bfloat16
    outputs = [jax.ShapeDtypeStruct(a.shape, f32) for a in arguments[5:8] + arguments[2:5]]
    vmem = pl.BlockSpec(memory_space=pltpu.VMEM)
    fulls = [(2, 1, S, WIDE[0]), (2, 2, S, WIDE[1]), (CHUNKS, 2, 3, S, WIDTH)]
    sends = [(PROCS, level, ROWS, 128) for level in (1, 2, 3)]
    turns = [(level, S, 128) for level in (1, 2, 3)]
    results = pl.pallas_call(
        kernel,
        out_shape=outputs,
        in_specs=[pl.BlockSpec(memory_space=pltpu.SMEM)] + [vmem] * 7,
        out_specs=[vmem] * 6,
        scratch_shapes=[pltpu.VMEM(shape, f32) for shape in fulls]
        + [pltpu.VMEM(shape, bf16) for shape in fulls]
        + [pltpu.VMEM(shape, bf16) for shape in fulls]
        + [
            pltpu.VMEM((2, 2, 3, ROWS, 3 * S), bf16),
            pltpu.VMEM((4, 2, ROWS, WIDE[0]), f32),
            pltpu.VMEM((2, 2, 2, ROWS, WIDE[1]), f32),
            pltpu.VMEM((2, 3, ROWS, S), f32),
            pltpu.VMEM((4, 2, ROWS, WIDE[0]), f32),
            pltpu.VMEM((2, 2, ROWS, WIDE[1]), f32),
        ]
        + [pltpu.VMEM(shape, f32) for shape in sends]
        + [pltpu.VMEM(shape, f32) for shape in turns]
        + [
            pltpu.SemaphoreType.DMA((2 + CHUNKS, 2, ROLES)),
            pltpu.SemaphoreType.DMA((2 + CHUNKS, 2, ROLES)),
            pltpu.SemaphoreType.DMA((5, 4)),
            pltpu.SemaphoreType.DMA((5, 4)),
            pltpu.SemaphoreType.DMA((4, PROCS)),
            pltpu.SemaphoreType.DMA((4, PROCS)),
        ],
        compiler_params=pltpu.CompilerParams(
            collective_id=0, has_side_effects=True, vmem_limit_bytes=62 * 2**20
        ),
    )(*arguments)
    return pl.pallas_call(
        hand_over,
        out_shape=outputs,
        in_specs=[vmem] * 6,
        out_specs=[vmem] * 6,
    )(*results)


def solution(mesh):
    in_specs = (
        P(),
        P(None, "proc", None),
        P(None, "proc", "group"),
        P(None, "proc", "group"),
        P(None, "proc", "group"),
        P(None, None, "proc", "group"),
        P(None, None, "proc", "group"),
        P(None, None, "proc", "group"),
    )
    out_specs = (
        P(None, None, "proc", "group"),
        P(None, None, "proc", "group"),
        P(None, None, "proc", "group"),
        P(None, "proc", "group"),
        P(None, "proc", "group"),
        P(None, "proc", "group"),
    )
    return jax.shard_map(shards, mesh=mesh, in_specs=in_specs, out_specs=out_specs, check_vma=False)
```

```python
import jax
import jax.numpy as jnp
from jax import lax
from jax.experimental import pallas as pl
from jax.experimental.pallas import tpu as pltpu
from jax.sharding import PartitionSpec as P

MESH = pl.DeviceIdType.MESH
S = 768
PROCS = 16
ROWS = S // PROCS
HALF = ROWS // 2
CHUNKS = 3
WIDTH = S // CHUNKS
WIDE = (256, 384)
COLS = (192, 384)
ROLES = 17
EXTRA = {ROWS: 8, 3 * ROWS: 32}
X_FIRST = ((2, 1), (3, 1))


def split(value):
    high = value.astype(jnp.bfloat16)
    low = (value - high.astype(jnp.float32)).astype(jnp.bfloat16)
    return high, low


def dot(first, second):
    return jnp.dot(first, second, preferred_element_type=jnp.float32)


def complex_rows(high, low, real_high, real_low, imag_high, imag_low):
    both = high.shape[0]
    half = both // 2
    stacked = jnp.concatenate([high, low], axis=0)
    by_real = dot(stacked, real_high)
    by_real = by_real[:both] + by_real[both:] + dot(high, real_low)
    by_imag = dot(stacked, imag_high)
    by_imag = by_imag[:both] + by_imag[both:] + dot(high, imag_low)
    return by_real[:half] - by_imag[half:], by_imag[:half] + by_real[half:]


def kernel(
    pattern,
    inverse_root,
    inverse_one,
    inverse_two,
    inverse_three,
    lower_one,
    lower_two,
    lower_three,
    upper_one,
    upper_two,
    upper_three,
    diagonal_one,
    diagonal_two,
    diagonal_three,
    full_one,
    full_two,
    full_three,
    high_one,
    high_two,
    high_three,
    low_one,
    low_two,
    low_three,
    chain,
    join_one,
    join_two,
    joined,
    join_diag_one,
    join_diag_two,
    send_one,
    send_two,
    send_three,
    got_one,
    got_two,
    got_three,
    turned_one,
    turned_two,
    turned_three,
    gather_send,
    gather_recv,
    join_send,
    join_recv,
    turn_send,
    turn_recv,
):
    group = lax.axis_index("group")
    me = lax.axis_index("proc")
    x_at = me // 4
    y_at = me // 2 % 2
    core = me % 2

    def proc_of(dx, dy, dc=0):
        return lax.rem(x_at + dx, 4) * 4 + lax.rem(y_at + dy, 2) * 2 + lax.rem(core + dc, 2)

    right, left = proc_of(1, 0), proc_of(3, 0)
    far, pair, sibling = proc_of(2, 0), proc_of(0, 1), proc_of(0, 0, 1)
    pair_right, pair_left, pair_far = proc_of(1, 1), proc_of(3, 1), proc_of(2, 1)

    barrier = pltpu.get_barrier_semaphore()
    for step in range(1, PROCS):
        pl.semaphore_signal(
            barrier, inc=1, device_id=(group, lax.rem(me + step, PROCS)), device_id_type=MESH
        )
    for flip in range(1, 4):
        pl.semaphore_signal(barrier, inc=1, device_id=(group ^ flip, me), device_id_type=MESH)

    def keep(level, a):
        node = group // 2 ** (3 - level)
        first = (level - 2) * 2**level + 2
        return pattern[first + node * level + a].astype(jnp.float32)

    buffers = [full_one, full_two] + [full_three.at[c] for c in range(CHUNKS)]
    highs = [high_one, high_two] + [high_three.at[c] for c in range(CHUNKS)]
    lows = [low_one, low_two] + [low_three.at[c] for c in range(CHUNKS)]

    def rows_of(proc, offset=0):
        return pl.multiple_of(proc * ROWS + offset, 8)

    own = pl.ds(rows_of(me), ROWS)

    def own_block(q):
        if q == 0:
            full_one[:, :, own, :] = jnp.zeros((2, 1, ROWS, WIDE[0]), jnp.float32)
            full_one[:, 0, own, : COLS[0]] = lower_one[:, 0] * keep(1, 0)
        elif q == 1:
            for a in range(2):
                full_two[:, a, own, :] = lower_two[:, a] * keep(2, a)
        else:
            columns = slice((q - 2) * WIDTH, (q - 1) * WIDTH)
            for a in range(3):
                full_three[q - 2, :, a, own, :] = lower_three[:, a, :, columns] * keep(3, a)

    own_block(0)
    own_block(1)
    pl.semaphore_wait(barrier, PROCS - 1 + 3)

    pending = []

    def block(chunk, part, proc, half):
        offset, count = (0, ROWS) if half is None else (half * HALF, HALF)
        return buffers[chunk].at[part, :, pl.ds(rows_of(proc, offset), count), :]

    def gather_copy(chunk, part, role, proc, to, half):
        place = block(chunk, part, proc, half)
        return pltpu.make_async_remote_copy(
            src_ref=place,
            dst_ref=place,
            send_sem=gather_send.at[chunk, part, role],
            recv_sem=gather_recv.at[chunk, part, role],
            device_id=(group, to),
            device_id_type=MESH,
        )

    def send(chunk, part, role, proc, to, half=None):
        copy = gather_copy(chunk, part, role, proc, to, half)
        copy.start()
        pending.append(copy)

    def arrive(chunk, part, role, proc, half=None):
        gather_copy(chunk, part, role, proc, sibling, half).wait_recv()

    def x_first(q, part):
        return (q, part) in X_FIRST

    def stage_a(q):
        if q > 1:
            own_block(q)
        for part in range(2):
            send(q, part, 0, me, pair)
        for part in range(2):
            send(q, part, 1, me, right)
            send(q, part, 2, me, left)
        for part in range(2):
            send(q, part, 9, me, sibling)

    def stage_b(q):
        for part in range(2):
            if not x_first(q, part):
                arrive(q, part, 0, pair)
                send(q, part, 3, pair, right)
                send(q, part, 4, pair, left)
                send(q, part, 10, pair, sibling)
        for part in range(2):
            arrive(q, part, 1, left)
            send(q, part, 5, left, right, 0)
            if x_first(q, part):
                send(q, part, 3, left, pair)
            send(q, part, 11, left, sibling)
            arrive(q, part, 2, right)
            send(q, part, 6, right, left, 1)
            if x_first(q, part):
                send(q, part, 4, right, pair)
            send(q, part, 12, right, sibling)

    def stage_c(q):
        for part in range(2):
            arrive(q, part, 5, far, 0)
            arrive(q, part, 6, far, 1)
            if x_first(q, part):
                send(q, part, 7, far, pair)
                arrive(q, part, 0, pair)
                send(q, part, 10, pair, sibling)
            send(q, part, 15, far, sibling)
        for part in range(2):
            if not x_first(q, part):
                arrive(q, part, 3, pair_left)
                send(q, part, 7, pair_left, right, 0)
                send(q, part, 13, pair_left, sibling)
                arrive(q, part, 4, pair_right)
                send(q, part, 8, pair_right, left, 1)
                send(q, part, 14, pair_right, sibling)

    def stage_d(q):
        for part in range(2):
            if x_first(q, part):
                arrive(q, part, 3, pair_left)
                send(q, part, 13, pair_left, sibling)
                arrive(q, part, 4, pair_right)
                send(q, part, 14, pair_right, sibling)
                arrive(q, part, 7, pair_far)
            else:
                arrive(q, part, 7, pair_far, 0)
                arrive(q, part, 8, pair_far, 1)
            send(q, part, 16, pair_far, sibling)

    def stage_e(q):
        flip = 1 - 2 * core
        sources = (me, pair, left, right, pair_left, pair_right, far, pair_far)
        for part in range(2):
            for at, proc in enumerate(sources):
                arrive(q, part, 9 + at, proc + flip)

    def convert(q):
        for part in range(2):
            for a in range(buffers[q].shape[1]):
                high, low = split(buffers[q][part, a])
                highs[q][part, a] = high
                lows[q][part, a] = low

    def factors(q):
        levels, width = highs[q].shape[1], highs[q].shape[3]
        return [
            ref[part].reshape(levels * S, width) for part in range(2) for ref in (highs[q], lows[q])
        ]

    def new_upper(q, level, first, last):
        depth = level * S
        rows = 2 * (last - first) * ROWS
        high = chain[0, :, first:last, :, :depth].reshape(rows, depth)
        low = chain[1, :, first:last, :, :depth].reshape(rows, depth)
        real, imag = complex_rows(high, low, *factors(q))
        shape = (last - first, ROWS, highs[q].shape[3])
        return -real.reshape(shape), -imag.reshape(shape)

    def join_copies(step, flips, ref, slot, at=()):
        copies = []
        for flip in flips:
            copy = pltpu.make_async_remote_copy(
                src_ref=ref.at[(slot, *at)],
                dst_ref=ref.at[(slot, *at)],
                send_sem=join_send.at[step, flip],
                recv_sem=join_recv.at[step, flip],
                device_id=(group ^ flip, me),
                device_id_type=MESH,
            )
            copy.start()
            copies.append(copy)
        pending.extend(copies)

    def join_waits(step, flips, ref, slot, at=()):
        for flip in flips:
            place = ref.at[(slot ^ flip, *at)]
            pltpu.make_async_remote_copy(
                src_ref=place,
                dst_ref=place,
                send_sem=join_send.at[step, flip],
                recv_sem=join_recv.at[step, flip],
                device_id=(group ^ flip, me),
                device_id_type=MESH,
            ).wait_recv()

    def widen(pieces):
        lane = lax.broadcasted_iota(jnp.int32, (pieces[0].shape[0], 128), 1)
        tiles = []
        for even, odd in ((pieces[0], pieces[1]), (pieces[2], pieces[3])):
            rolled = pltpu.roll(odd, 64, 1)
            tiles += [
                even[:, :128],
                jnp.where(lane < 64, even[:, 128:], rolled[:, :128]),
                rolled[:, 128:],
            ]
        return jnp.concatenate(tiles, axis=1)

    def window(real, imag, proc, base=0):
        start = proc * ROWS - base
        tile, shift = start // 128 * 128, start % 128
        count = 128 if shift + ROWS <= 128 else 256
        lane = lax.broadcasted_iota(jnp.int32, (real.shape[0], 128), 1)
        first = real[:, tile : tile + count]
        second = imag[:, tile : tile + count]
        if shift:
            first = pltpu.roll(first, count - shift, 1)[:, :128]
        if shift != ROWS:
            second = pltpu.roll(second, (count + ROWS - shift) % count, 1)[:, :128]
        return jnp.where(lane < ROWS, first[:, :128], second[:, :128])

    def pack(value):
        extra = EXTRA[value.shape[0]]
        kept = value.shape[0] - extra
        lane = lax.broadcasted_iota(jnp.int32, (extra, 128), 1)
        spare = value[kept:]
        parts = [
            jnp.where(
                lane < 2 * ROWS,
                value[t * extra : (t + 1) * extra],
                pltpu.roll(spare, 2 * ROWS - 32 * t, 1),
            )
            for t in range(3)
        ]
        return jnp.concatenate(parts + [value[3 * extra : kept]], axis=0)

    def unpack(value, count):
        extra = EXTRA[count]
        lane = lax.broadcasted_iota(jnp.int32, (extra, 128), 1)
        parts = [
            pltpu.roll(value[t * extra : (t + 1) * extra], 32 * t + 32, 1) for t in range(3)
        ]
        spare = jnp.where(lane < 32, parts[0], jnp.where(lane < 64, parts[1], parts[2]))
        return jnp.concatenate([value, spare], axis=0)

    def turn_copy(turn, source, target, to):
        return pltpu.make_async_remote_copy(
            src_ref=source.at[to],
            dst_ref=target.at[me],
            send_sem=turn_send.at[turn, to],
            recv_sem=turn_recv.at[turn, me],
            device_id=(group, to),
            device_id_type=MESH,
        )

    def turn_arrive(turn, source, target, proc):
        pltpu.make_async_remote_copy(
            src_ref=source.at[proc],
            dst_ref=target.at[proc],
            send_sem=turn_send.at[turn, proc],
            recv_sem=turn_recv.at[turn, proc],
            device_id=(group, proc),
            device_id_type=MESH,
        ).wait_recv()

    def fill(source, first, last, proc):
        rows = (last - first) * ROWS
        real = joined[0, first:last].reshape(rows, S)
        imag = joined[1, first:last].reshape(rows, S)
        source[proc] = pack(window(real, imag, proc))

    def turn_start(turn, source, target, first, last):
        for proc in range(PROCS):
            fill(source, first, last, proc)
        for step in range(1, PROCS):
            copy = turn_copy(turn, source, target, lax.rem(me + step, PROCS))
            copy.start()
            pending.append(copy)
        target[me] = source[me]

    def turn_wait(turn, source, target, turned, first, last):
        for step in range(1, PROCS):
            turn_arrive(turn, source, target, lax.rem(me + PROCS - step, PROCS))
        for proc in range(PROCS):
            value = unpack(target[proc], (last - first) * ROWS)
            rows = slice(proc * ROWS, (proc + 1) * ROWS)
            turned[first:last, rows, :] = value.reshape(last - first, ROWS, 128)

    def turned_rows(target):
        flat = target[...].reshape(target.shape[0] * S, 128)
        return split(flat.T[: 2 * ROWS])

    def new_diagonal(q, row_high, row_low):
        return complex_rows(row_high, row_low, *factors(q))

    def put_chain(part, a, columns, value):
        high, low = split(value)
        chain[0, part, a, :, columns] = high
        chain[1, part, a, :, columns] = low

    slot_one, slot_two = lax.rem(group, 4), lax.rem(group, 2)
    flips_one, flips_two = (1, 2, 3), (1,)

    stage_a(0)
    stage_a(1)
    stage_b(0)
    stage_a(2)
    stage_c(0)
    stage_b(1)
    stage_d(0)
    stage_e(0)
    for part in range(2):
        high, low = split(inverse_root[part])
        chain[0, part, 0, :, :S] = high
        chain[1, part, 0, :, :S] = low
    convert(0)
    real, imag = new_upper(0, 1, 0, 1)
    for part, value in ((0, real), (1, imag)):
        upper_one[part] = value[:, :, : COLS[0]]
        join_one[slot_one, part] = value[0]
    join_copies(0, flips_one, join_one, slot_one)
    stage_a(3)
    stage_c(1)
    stage_b(2)
    join_waits(0, flips_one, join_one, slot_one)
    for part in range(2):
        value = widen([join_one[j, part] for j in range(4)])
        joined[part, 0] = value
        put_chain(part, 0, slice(S, 2 * S), value)
    turn_start(0, send_one, got_one, 0, 1)
    stage_d(1)
    stage_a(4)
    turn_wait(0, send_one, got_one, turned_one, 0, 1)
    row_high, row_low = turned_rows(turned_one)
    for part in range(2):
        rows = slice(part * ROWS, (part + 1) * ROWS)
        chain[0, part, 1, :, :S] = row_high[rows]
        chain[1, part, 1, :, :S] = row_low[rows]
    product = new_diagonal(0, row_high, row_low)
    for part in range(2):
        value = inverse_one[part] - product[part][:, : COLS[0]]
        diagonal_one[part] = value
        join_diag_one[slot_one, part, :, : COLS[0]] = value
    join_copies(1, flips_one, join_diag_one, slot_one)
    stage_c(2)
    stage_b(3)
    stage_e(1)

    convert(1)

    def upper_two_rows(a):
        real, imag = new_upper(1, 2, a, a + 1)
        for part, value in ((0, real), (1, imag)):
            upper_two[part, a] = value[0]
            join_two[slot_two, part, a] = value[0]
        join_copies(2 + a, flips_two, join_two, slot_two, (slice(None), a))

    def join_two_rows(a):
        join_waits(2 + a, flips_two, join_two, slot_two, (slice(None), a))
        for part in range(2):
            for j in range(2):
                value = join_two[j, part, a]
                joined[part, a, :, j * COLS[1] : (j + 1) * COLS[1]] = value
                put_chain(part, a, slice(2 * S + j * COLS[1], 2 * S + (j + 1) * COLS[1]), value)
        turn_start(1 + a, send_two.at[a], got_two.at[a], a, a + 1)

    upper_two_rows(0)
    join_waits(1, flips_one, join_diag_one, slot_one)
    for part in range(2):
        value = widen([join_diag_one[j, part] for j in range(4)])
        put_chain(part, 1, slice(S, 2 * S), value)
    upper_two_rows(1)
    join_two_rows(0)
    stage_d(2)
    stage_c(3)
    join_two_rows(1)
    stage_b(4)
    stage_e(2)

    def upper_three_rows(c, first, last):
        real, imag = new_upper(2 + c, 3, first, last)
        columns = slice(c * WIDTH, (c + 1) * WIDTH)
        for part, value in ((0, real), (1, imag)):
            upper_three[part, first:last, :, columns] = value
            joined[part, first:last, :, columns] = value

    def turn_three(c):
        for proc in range(c * WIDTH // ROWS, (c + 1) * WIDTH // ROWS):
            fill(send_three, 0, 3, proc)

            @pl.when(me != proc)
            def _():
                turn_copy(3, send_three, got_three, proc).start()

    convert(2)
    upper_three_rows(0, 0, 2)
    for a in range(2):
        turn_wait(1 + a, send_two.at[a], got_two.at[a], turned_two, a, a + 1)
    row_high, row_low = turned_rows(turned_two)
    for part in range(2):
        rows = slice(part * ROWS, (part + 1) * ROWS)
        chain[0, part, 2, :, : 2 * S] = row_high[rows]
        chain[1, part, 2, :, : 2 * S] = row_low[rows]
    product = new_diagonal(1, row_high, row_low)
    for part in range(2):
        value = inverse_two[part] - product[part]
        diagonal_two[part] = value
        join_diag_two[slot_two, part] = value
    join_copies(4, flips_two, join_diag_two, slot_two)
    stage_d(3)
    stage_c(4)
    stage_e(3)
    convert(3)
    upper_three_rows(1, 0, 2)
    join_waits(4, flips_two, join_diag_two, slot_two)
    for part in range(2):
        for j in range(2):
            put_chain(
                part,
                2,
                slice(2 * S + j * COLS[1], 2 * S + (j + 1) * COLS[1]),
                join_diag_two[j, part],
            )
    upper_three_rows(0, 2, 3)
    turn_three(0)
    stage_d(4)
    upper_three_rows(1, 2, 3)
    turn_three(1)
    stage_e(4)
    convert(4)
    upper_three_rows(2, 0, 3)
    turn_three(2)
    got_three[me] = send_three[me]
    turn_wait(3, send_three, got_three, turned_three, 0, 3)
    row_high, row_low = turned_rows(turned_three)
    for c in range(CHUNKS):
        columns = slice(c * WIDTH, (c + 1) * WIDTH)
        product = new_diagonal(2 + c, row_high, row_low)
        for part in range(2):
            diagonal_three[part, :, columns] = inverse_three[part, :, columns] - product[part]

    for copy in pending:
        copy.wait_send()
    for step in range(1, PROCS):
        to = lax.rem(me + step, PROCS)
        turn_copy(3, send_three, got_three, to).wait_send()


def hand_over(*refs):
    for at in range(6):
        refs[at + 6][...] = refs[at][...]


def shards(*arguments):
    f32, bf16 = jnp.float32, jnp.bfloat16
    outputs = [jax.ShapeDtypeStruct(a.shape, f32) for a in arguments[5:8] + arguments[2:5]]
    vmem = pl.BlockSpec(memory_space=pltpu.VMEM)
    fulls = [(2, 1, S, WIDE[0]), (2, 2, S, WIDE[1]), (CHUNKS, 2, 3, S, WIDTH)]
    counts = [level * ROWS - EXTRA[level * ROWS] for level in (1, 3)]
    sends = [
        (PROCS, counts[0], 128),
        (2, PROCS, counts[0], 128),
        (PROCS, counts[1], 128),
    ]
    turns = [(level, S, 128) for level in (1, 2, 3)]
    results = pl.pallas_call(
        kernel,
        out_shape=outputs,
        in_specs=[pl.BlockSpec(memory_space=pltpu.SMEM)] + [vmem] * 7,
        out_specs=[vmem] * 6,
        scratch_shapes=[pltpu.VMEM(shape, f32) for shape in fulls]
        + [pltpu.VMEM(shape, bf16) for shape in fulls]
        + [pltpu.VMEM(shape, bf16) for shape in fulls]
        + [
            pltpu.VMEM((2, 2, 3, ROWS, 3 * S), bf16),
            pltpu.VMEM((4, 2, ROWS, WIDE[0]), f32),
            pltpu.VMEM((2, 2, 2, ROWS, WIDE[1]), f32),
            pltpu.VMEM((2, 3, ROWS, S), f32),
            pltpu.VMEM((4, 2, ROWS, WIDE[0]), f32),
            pltpu.VMEM((2, 2, ROWS, WIDE[1]), f32),
        ]
        + [pltpu.VMEM(shape, f32) for shape in sends]
        + [pltpu.VMEM(shape, f32) for shape in sends]
        + [pltpu.VMEM(shape, f32) for shape in turns]
        + [
            pltpu.SemaphoreType.DMA((2 + CHUNKS, 2, ROLES)),
            pltpu.SemaphoreType.DMA((2 + CHUNKS, 2, ROLES)),
            pltpu.SemaphoreType.DMA((5, 4)),
            pltpu.SemaphoreType.DMA((5, 4)),
            pltpu.SemaphoreType.DMA((4, PROCS)),
            pltpu.SemaphoreType.DMA((4, PROCS)),
        ],
        compiler_params=pltpu.CompilerParams(
            collective_id=0, has_side_effects=True, vmem_limit_bytes=62 * 2**20
        ),
    )(*arguments)
    return pl.pallas_call(
        hand_over,
        out_shape=outputs,
        in_specs=[vmem] * 6,
        out_specs=[vmem] * 6,
    )(*results)


def solution(mesh):
    in_specs = (
        P(),
        P(None, "proc", None),
        P(None, "proc", "group"),
        P(None, "proc", "group"),
        P(None, "proc", "group"),
        P(None, None, "proc", "group"),
        P(None, None, "proc", "group"),
        P(None, None, "proc", "group"),
    )
    out_specs = (
        P(None, None, "proc", "group"),
        P(None, None, "proc", "group"),
        P(None, None, "proc", "group"),
        P(None, "proc", "group"),
        P(None, "proc", "group"),
        P(None, "proc", "group"),
    )
    return jax.shard_map(shards, mesh=mesh, in_specs=in_specs, out_specs=out_specs, check_vma=False)
```

```python
import jax
import jax.numpy as jnp
from jax import lax
from jax.experimental import pallas as pl
from jax.experimental.pallas import tpu as pltpu
from jax.sharding import PartitionSpec as P

MESH = pl.DeviceIdType.MESH
S = 768
PROCS = 16
ROWS = S // PROCS
HALF = ROWS // 2
CHUNKS = 3
WIDTH = S // CHUNKS
WIDE = (256, 384)
COLS = (192, 384)
ROLES = 17
EXTRA = {ROWS: 8, 3 * ROWS: 32}
X_FIRST = ((2, 1), (3, 1))


def split(value):
    high = value.astype(jnp.bfloat16)
    low = (value - high.astype(jnp.float32)).astype(jnp.bfloat16)
    return high, low


def dot(first, second):
    return jnp.dot(first, second, preferred_element_type=jnp.float32)


def complex_rows(high, low, real_high, real_low, imag_high, imag_low):
    both = high.shape[0]
    half = both // 2
    stacked = jnp.concatenate([high, low], axis=0)
    by_real = dot(stacked, real_high)
    by_real = by_real[:both] + by_real[both:] + dot(high, real_low)
    by_imag = dot(stacked, imag_high)
    by_imag = by_imag[:both] + by_imag[both:] + dot(high, imag_low)
    return by_real[:half] - by_imag[half:], by_imag[:half] + by_real[half:]


def kernel(
    pattern,
    inverse_root,
    inverse_one,
    inverse_two,
    inverse_three,
    lower_one,
    lower_two,
    lower_three,
    upper_one,
    upper_two,
    upper_three,
    diagonal_one,
    diagonal_two,
    diagonal_three,
    full_one,
    full_two,
    full_three,
    high_one,
    high_two,
    high_three,
    low_one,
    low_two,
    low_three,
    chain,
    join_one,
    join_two,
    joined,
    join_diag_one,
    join_diag_two,
    send_one,
    send_two,
    send_three,
    got_one,
    got_two,
    got_three,
    turned_one,
    turned_two,
    turned_three,
    gather_send,
    gather_recv,
    join_send,
    join_recv,
    turn_send,
    turn_recv,
):
    group = lax.axis_index("group")
    me = lax.axis_index("proc")
    x_at = me // 4
    y_at = me // 2 % 2
    core = me % 2

    def proc_of(dx, dy, dc=0):
        return lax.rem(x_at + dx, 4) * 4 + lax.rem(y_at + dy, 2) * 2 + lax.rem(core + dc, 2)

    right, left = proc_of(1, 0), proc_of(3, 0)
    far, pair, sibling = proc_of(2, 0), proc_of(0, 1), proc_of(0, 0, 1)
    pair_right, pair_left, pair_far = proc_of(1, 1), proc_of(3, 1), proc_of(2, 1)

    barrier = pltpu.get_barrier_semaphore()
    for step in range(1, PROCS):
        pl.semaphore_signal(
            barrier, inc=1, device_id=(group, lax.rem(me + step, PROCS)), device_id_type=MESH
        )
    for flip in range(1, 4):
        pl.semaphore_signal(barrier, inc=1, device_id=(group ^ flip, me), device_id_type=MESH)

    def keep(level, a):
        node = group // 2 ** (3 - level)
        first = (level - 2) * 2**level + 2
        return pattern[first + node * level + a].astype(jnp.float32)

    buffers = [full_one, full_two] + [full_three.at[c] for c in range(CHUNKS)]
    highs = [high_one, high_two] + [high_three.at[c] for c in range(CHUNKS)]
    lows = [low_one, low_two] + [low_three.at[c] for c in range(CHUNKS)]

    def rows_of(proc, offset=0):
        return pl.multiple_of(proc * ROWS + offset, 8)

    own = pl.ds(rows_of(me), ROWS)

    def own_block(q):
        if q == 0:
            full_one[:, :, own, :] = jnp.zeros((2, 1, ROWS, WIDE[0]), jnp.float32)
            full_one[:, 0, own, : COLS[0]] = lower_one[:, 0] * keep(1, 0)
        elif q == 1:
            for a in range(2):
                full_two[:, a, own, :] = lower_two[:, a] * keep(2, a)
        else:
            columns = slice((q - 2) * WIDTH, (q - 1) * WIDTH)
            for a in range(3):
                full_three[q - 2, :, a, own, :] = lower_three[:, a, :, columns] * keep(3, a)

    own_block(0)
    own_block(1)
    pl.semaphore_wait(barrier, PROCS - 1 + 3)

    pending = []

    def block(chunk, part, proc, half):
        offset, count = (0, ROWS) if half is None else (half * HALF, HALF)
        return buffers[chunk].at[part, :, pl.ds(rows_of(proc, offset), count), :]

    def gather_copy(chunk, part, role, proc, to, half):
        place = block(chunk, part, proc, half)
        return pltpu.make_async_remote_copy(
            src_ref=place,
            dst_ref=place,
            send_sem=gather_send.at[chunk, part, role],
            recv_sem=gather_recv.at[chunk, part, role],
            device_id=(group, to),
            device_id_type=MESH,
        )

    def send(chunk, part, role, proc, to, half=None):
        copy = gather_copy(chunk, part, role, proc, to, half)
        copy.start()
        pending.append(copy)

    def arrive(chunk, part, role, proc, half=None):
        gather_copy(chunk, part, role, proc, sibling, half).wait_recv()

    def x_first(q, part):
        return (q, part) in X_FIRST

    def stage_a(q):
        if q > 1:
            own_block(q)
        for part in range(2):
            send(q, part, 0, me, pair)
        for part in range(2):
            send(q, part, 1, me, right)
            send(q, part, 2, me, left)
        for part in range(2):
            send(q, part, 9, me, sibling)

    def stage_b(q):
        for part in range(2):
            if not x_first(q, part):
                arrive(q, part, 0, pair)
                send(q, part, 3, pair, right)
                send(q, part, 4, pair, left)
                send(q, part, 10, pair, sibling)
        for part in range(2):
            arrive(q, part, 1, left)
            send(q, part, 5, left, right, 0)
            if x_first(q, part):
                send(q, part, 3, left, pair)
            send(q, part, 11, left, sibling)
            arrive(q, part, 2, right)
            send(q, part, 6, right, left, 1)
            if x_first(q, part):
                send(q, part, 4, right, pair)
            send(q, part, 12, right, sibling)

    def stage_c(q):
        for part in range(2):
            arrive(q, part, 5, far, 0)
            arrive(q, part, 6, far, 1)
            if x_first(q, part):
                send(q, part, 7, far, pair)
                arrive(q, part, 0, pair)
                send(q, part, 10, pair, sibling)
            send(q, part, 15, far, sibling)
        for part in range(2):
            if not x_first(q, part):
                arrive(q, part, 3, pair_left)
                send(q, part, 7, pair_left, right, 0)
                send(q, part, 13, pair_left, sibling)
                arrive(q, part, 4, pair_right)
                send(q, part, 8, pair_right, left, 1)
                send(q, part, 14, pair_right, sibling)

    def stage_d(q):
        for part in range(2):
            if x_first(q, part):
                arrive(q, part, 3, pair_left)
                send(q, part, 13, pair_left, sibling)
                arrive(q, part, 4, pair_right)
                send(q, part, 14, pair_right, sibling)
                arrive(q, part, 7, pair_far)
            else:
                arrive(q, part, 7, pair_far, 0)
                arrive(q, part, 8, pair_far, 1)
            send(q, part, 16, pair_far, sibling)

    def stage_e(q):
        flip = 1 - 2 * core
        sources = (me, pair, left, right, pair_left, pair_right, far, pair_far)
        for part in range(2):
            for at, proc in enumerate(sources):
                arrive(q, part, 9 + at, proc + flip)

    def convert(q):
        for part in range(2):
            for a in range(buffers[q].shape[1]):
                high, low = split(buffers[q][part, a])
                highs[q][part, a] = high
                lows[q][part, a] = low

    def factors(q):
        levels, width = highs[q].shape[1], highs[q].shape[3]
        return [
            ref[part].reshape(levels * S, width) for part in range(2) for ref in (highs[q], lows[q])
        ]

    def new_upper(q, level, first, last):
        depth = level * S
        rows = 2 * (last - first) * ROWS
        high = chain[0, :, first:last, :, :depth].reshape(rows, depth)
        low = chain[1, :, first:last, :, :depth].reshape(rows, depth)
        real, imag = complex_rows(high, low, *factors(q))
        shape = (last - first, ROWS, highs[q].shape[3])
        return -real.reshape(shape), -imag.reshape(shape)

    def join_copies(step, flips, ref, slot, at=()):
        copies = []
        for flip in flips:
            copy = pltpu.make_async_remote_copy(
                src_ref=ref.at[(slot, *at)],
                dst_ref=ref.at[(slot, *at)],
                send_sem=join_send.at[step, flip],
                recv_sem=join_recv.at[step, flip],
                device_id=(group ^ flip, me),
                device_id_type=MESH,
            )
            copy.start()
            copies.append(copy)
        pending.extend(copies)

    def join_waits(step, flips, ref, slot, at=()):
        for flip in flips:
            place = ref.at[(slot ^ flip, *at)]
            pltpu.make_async_remote_copy(
                src_ref=place,
                dst_ref=place,
                send_sem=join_send.at[step, flip],
                recv_sem=join_recv.at[step, flip],
                device_id=(group ^ flip, me),
                device_id_type=MESH,
            ).wait_recv()

    def widen(pieces):
        lane = lax.broadcasted_iota(jnp.int32, (pieces[0].shape[0], 128), 1)
        tiles = []
        for even, odd in ((pieces[0], pieces[1]), (pieces[2], pieces[3])):
            rolled = pltpu.roll(odd, 64, 1)
            tiles += [
                even[:, :128],
                jnp.where(lane < 64, even[:, 128:], rolled[:, :128]),
                rolled[:, 128:],
            ]
        return jnp.concatenate(tiles, axis=1)

    def window(real, imag, proc, base=0):
        start = proc * ROWS - base
        tile, shift = start // 128 * 128, start % 128
        count = 128 if shift + ROWS <= 128 else 256
        lane = lax.broadcasted_iota(jnp.int32, (real.shape[0], 128), 1)
        first = real[:, tile : tile + count]
        second = imag[:, tile : tile + count]
        if shift:
            first = pltpu.roll(first, count - shift, 1)[:, :128]
        if shift != ROWS:
            second = pltpu.roll(second, (count + ROWS - shift) % count, 1)[:, :128]
        return jnp.where(lane < ROWS, first[:, :128], second[:, :128])

    def pack(value):
        extra = EXTRA[value.shape[0]]
        kept = value.shape[0] - extra
        lane = lax.broadcasted_iota(jnp.int32, (extra, 128), 1)
        spare = value[kept:]
        parts = [
            jnp.where(
                lane < 2 * ROWS,
                value[t * extra : (t + 1) * extra],
                pltpu.roll(spare, 2 * ROWS - 32 * t, 1),
            )
            for t in range(3)
        ]
        return jnp.concatenate(parts + [value[3 * extra : kept]], axis=0)

    def unpack(value, count):
        extra = EXTRA[count]
        lane = lax.broadcasted_iota(jnp.int32, (extra, 128), 1)
        parts = [
            pltpu.roll(value[t * extra : (t + 1) * extra], 32 * t + 32, 1) for t in range(3)
        ]
        spare = jnp.where(lane < 32, parts[0], jnp.where(lane < 64, parts[1], parts[2]))
        return jnp.concatenate([value, spare], axis=0)

    def turn_copy(turn, source, target, to):
        return pltpu.make_async_remote_copy(
            src_ref=source.at[to],
            dst_ref=target.at[me],
            send_sem=turn_send.at[turn, to],
            recv_sem=turn_recv.at[turn, me],
            device_id=(group, to),
            device_id_type=MESH,
        )

    def turn_arrive(turn, source, target, proc):
        pltpu.make_async_remote_copy(
            src_ref=source.at[proc],
            dst_ref=target.at[proc],
            send_sem=turn_send.at[turn, proc],
            recv_sem=turn_recv.at[turn, proc],
            device_id=(group, proc),
            device_id_type=MESH,
        ).wait_recv()

    def fill(source, first, last, proc):
        rows = (last - first) * ROWS
        real = joined[0, first:last].reshape(rows, S)
        imag = joined[1, first:last].reshape(rows, S)
        source[proc] = pack(window(real, imag, proc))

    def turn_start(turn, source, target, first, last):
        for proc in range(PROCS):
            fill(source, first, last, proc)
        for step in range(1, PROCS):
            copy = turn_copy(turn, source, target, lax.rem(me + step, PROCS))
            copy.start()
            pending.append(copy)
        target[me] = source[me]

    def turn_wait(turn, source, target, turned, first, last):
        for step in range(PROCS):
            proc = lax.rem(me + PROCS - step, PROCS)
            if step:
                turn_arrive(turn, source, target, proc)
            value = unpack(target[proc], (last - first) * ROWS)
            rows = pl.ds(rows_of(proc), ROWS)
            turned[first:last, rows, :] = value.reshape(last - first, ROWS, 128)

    def turned_rows(target):
        flat = target[...].reshape(target.shape[0] * S, 128)
        return split(flat.T[: 2 * ROWS])

    def new_diagonal(q, row_high, row_low):
        return complex_rows(row_high, row_low, *factors(q))

    def put_chain(part, a, columns, value):
        high, low = split(value)
        chain[0, part, a, :, columns] = high
        chain[1, part, a, :, columns] = low

    slot_one, slot_two = lax.rem(group, 4), lax.rem(group, 2)
    flips_one, flips_two = (1, 2, 3), (1,)

    stage_a(0)
    stage_a(1)
    stage_b(0)
    stage_a(2)
    stage_c(0)
    stage_b(1)
    stage_d(0)
    stage_e(0)
    for part in range(2):
        high, low = split(inverse_root[part])
        chain[0, part, 0, :, :S] = high
        chain[1, part, 0, :, :S] = low
    convert(0)
    real, imag = new_upper(0, 1, 0, 1)
    for part, value in ((0, real), (1, imag)):
        upper_one[part] = value[:, :, : COLS[0]]
        join_one[slot_one, part] = value[0]
    join_copies(0, flips_one, join_one, slot_one)
    stage_a(3)
    stage_c(1)
    stage_b(2)
    join_waits(0, flips_one, join_one, slot_one)
    for part in range(2):
        value = widen([join_one[j, part] for j in range(4)])
        joined[part, 0] = value
        put_chain(part, 0, slice(S, 2 * S), value)
    turn_start(0, send_one, got_one, 0, 1)
    stage_d(1)
    stage_a(4)
    turn_wait(0, send_one, got_one, turned_one, 0, 1)
    row_high, row_low = turned_rows(turned_one)
    for part in range(2):
        rows = slice(part * ROWS, (part + 1) * ROWS)
        chain[0, part, 1, :, :S] = row_high[rows]
        chain[1, part, 1, :, :S] = row_low[rows]
    product = new_diagonal(0, row_high, row_low)
    for part in range(2):
        value = inverse_one[part] - product[part][:, : COLS[0]]
        diagonal_one[part] = value
        join_diag_one[slot_one, part, :, : COLS[0]] = value
    join_copies(1, flips_one, join_diag_one, slot_one)
    stage_c(2)
    stage_b(3)
    stage_e(1)

    convert(1)

    def upper_two_rows(a):
        real, imag = new_upper(1, 2, a, a + 1)
        for part, value in ((0, real), (1, imag)):
            upper_two[part, a] = value[0]
            join_two[slot_two, part, a] = value[0]
        join_copies(2 + a, flips_two, join_two, slot_two, (slice(None), a))

    def join_two_rows(a):
        join_waits(2 + a, flips_two, join_two, slot_two, (slice(None), a))
        for part in range(2):
            for j in range(2):
                value = join_two[j, part, a]
                joined[part, a, :, j * COLS[1] : (j + 1) * COLS[1]] = value
                put_chain(part, a, slice(2 * S + j * COLS[1], 2 * S + (j + 1) * COLS[1]), value)
        turn_start(1 + a, send_two.at[a], got_two.at[a], a, a + 1)

    upper_two_rows(0)
    join_waits(1, flips_one, join_diag_one, slot_one)
    for part in range(2):
        value = widen([join_diag_one[j, part] for j in range(4)])
        put_chain(part, 1, slice(S, 2 * S), value)
    upper_two_rows(1)
    join_two_rows(0)
    stage_d(2)
    stage_c(3)
    join_two_rows(1)
    stage_b(4)
    stage_e(2)

    def upper_three_rows(c, first, last):
        real, imag = new_upper(2 + c, 3, first, last)
        columns = slice(c * WIDTH, (c + 1) * WIDTH)
        for part, value in ((0, real), (1, imag)):
            upper_three[part, first:last, :, columns] = value
            joined[part, first:last, :, columns] = value

    def turn_three(c):
        for proc in range(c * WIDTH // ROWS, (c + 1) * WIDTH // ROWS):
            fill(send_three, 0, 3, proc)

            @pl.when(me != proc)
            def _():
                turn_copy(3, send_three, got_three, proc).start()

    convert(2)
    upper_three_rows(0, 0, 2)
    for a in range(2):
        turn_wait(1 + a, send_two.at[a], got_two.at[a], turned_two, a, a + 1)
    row_high, row_low = turned_rows(turned_two)
    for part in range(2):
        rows = slice(part * ROWS, (part + 1) * ROWS)
        chain[0, part, 2, :, : 2 * S] = row_high[rows]
        chain[1, part, 2, :, : 2 * S] = row_low[rows]
    product = new_diagonal(1, row_high, row_low)
    for part in range(2):
        value = inverse_two[part] - product[part]
        diagonal_two[part] = value
        join_diag_two[slot_two, part] = value
    join_copies(4, flips_two, join_diag_two, slot_two)
    stage_d(3)
    stage_c(4)
    stage_e(3)
    convert(3)
    upper_three_rows(1, 0, 2)
    join_waits(4, flips_two, join_diag_two, slot_two)
    for part in range(2):
        for j in range(2):
            put_chain(
                part,
                2,
                slice(2 * S + j * COLS[1], 2 * S + (j + 1) * COLS[1]),
                join_diag_two[j, part],
            )
    upper_three_rows(0, 2, 3)
    turn_three(0)
    stage_d(4)
    upper_three_rows(1, 2, 3)
    turn_three(1)
    stage_e(4)
    convert(4)
    upper_three_rows(2, 0, 3)
    turn_three(2)
    got_three[me] = send_three[me]
    turn_wait(3, send_three, got_three, turned_three, 0, 3)
    row_high, row_low = turned_rows(turned_three)
    for c in range(CHUNKS):
        columns = slice(c * WIDTH, (c + 1) * WIDTH)
        product = new_diagonal(2 + c, row_high, row_low)
        for part in range(2):
            diagonal_three[part, :, columns] = inverse_three[part, :, columns] - product[part]

    for copy in pending:
        copy.wait_send()
    for step in range(1, PROCS):
        to = lax.rem(me + step, PROCS)
        turn_copy(3, send_three, got_three, to).wait_send()


def hand_over(*refs):
    for at in range(6):
        refs[at + 6][...] = refs[at][...]


def shards(*arguments):
    f32, bf16 = jnp.float32, jnp.bfloat16
    outputs = [jax.ShapeDtypeStruct(a.shape, f32) for a in arguments[5:8] + arguments[2:5]]
    vmem = pl.BlockSpec(memory_space=pltpu.VMEM)
    fulls = [(2, 1, S, WIDE[0]), (2, 2, S, WIDE[1]), (CHUNKS, 2, 3, S, WIDTH)]
    counts = [level * ROWS - EXTRA[level * ROWS] for level in (1, 3)]
    sends = [
        (PROCS, counts[0], 128),
        (2, PROCS, counts[0], 128),
        (PROCS, counts[1], 128),
    ]
    turns = [(level, S, 128) for level in (1, 2, 3)]
    results = pl.pallas_call(
        kernel,
        out_shape=outputs,
        in_specs=[pl.BlockSpec(memory_space=pltpu.SMEM)] + [vmem] * 7,
        out_specs=[vmem] * 6,
        scratch_shapes=[pltpu.VMEM(shape, f32) for shape in fulls]
        + [pltpu.VMEM(shape, bf16) for shape in fulls]
        + [pltpu.VMEM(shape, bf16) for shape in fulls]
        + [
            pltpu.VMEM((2, 2, 3, ROWS, 3 * S), bf16),
            pltpu.VMEM((4, 2, ROWS, WIDE[0]), f32),
            pltpu.VMEM((2, 2, 2, ROWS, WIDE[1]), f32),
            pltpu.VMEM((2, 3, ROWS, S), f32),
            pltpu.VMEM((4, 2, ROWS, WIDE[0]), f32),
            pltpu.VMEM((2, 2, ROWS, WIDE[1]), f32),
        ]
        + [pltpu.VMEM(shape, f32) for shape in sends]
        + [pltpu.VMEM(shape, f32) for shape in sends]
        + [pltpu.VMEM(shape, f32) for shape in turns]
        + [
            pltpu.SemaphoreType.DMA((2 + CHUNKS, 2, ROLES)),
            pltpu.SemaphoreType.DMA((2 + CHUNKS, 2, ROLES)),
            pltpu.SemaphoreType.DMA((5, 4)),
            pltpu.SemaphoreType.DMA((5, 4)),
            pltpu.SemaphoreType.DMA((4, PROCS)),
            pltpu.SemaphoreType.DMA((4, PROCS)),
        ],
        compiler_params=pltpu.CompilerParams(
            collective_id=0, has_side_effects=True, vmem_limit_bytes=62 * 2**20
        ),
    )(*arguments)
    return pl.pallas_call(
        hand_over,
        out_shape=outputs,
        in_specs=[vmem] * 6,
        out_specs=[vmem] * 6,
    )(*results)


def solution(mesh):
    in_specs = (
        P(),
        P(None, "proc", None),
        P(None, "proc", "group"),
        P(None, "proc", "group"),
        P(None, "proc", "group"),
        P(None, None, "proc", "group"),
        P(None, None, "proc", "group"),
        P(None, None, "proc", "group"),
    )
    out_specs = (
        P(None, None, "proc", "group"),
        P(None, None, "proc", "group"),
        P(None, None, "proc", "group"),
        P(None, "proc", "group"),
        P(None, "proc", "group"),
        P(None, "proc", "group"),
    )
    return jax.shard_map(shards, mesh=mesh, in_specs=in_specs, out_specs=out_specs, check_vma=False)
```

```python
import jax
import jax.numpy as jnp
from jax import lax
from jax.experimental import pallas as pl
from jax.experimental.pallas import tpu as pltpu
from jax.sharding import PartitionSpec as P

MESH = pl.DeviceIdType.MESH
S = 768
PROCS = 16
ROWS = S // PROCS
HALF = ROWS // 2
CHUNKS = 3
WIDTH = S // CHUNKS
WIDE = (256, 384)
COLS = (192, 384)
ROLES = 17
EXTRA = {ROWS: 8, 3 * ROWS: 32}
X_FIRST = ((2, 1), (3, 1))


def split(value):
    high = value.astype(jnp.bfloat16)
    low = (value - high.astype(jnp.float32)).astype(jnp.bfloat16)
    return high, low


def dot(first, second):
    return jnp.dot(first, second, preferred_element_type=jnp.float32)


def complex_rows(high, low, real_high, real_low, imag_high, imag_low):
    both = high.shape[0]
    half = both // 2
    stacked = jnp.concatenate([high, low], axis=0)
    by_real = dot(stacked, real_high)
    by_real = by_real[:both] + by_real[both:] + dot(high, real_low)
    by_imag = dot(stacked, imag_high)
    by_imag = by_imag[:both] + by_imag[both:] + dot(high, imag_low)
    return by_real[:half] - by_imag[half:], by_imag[:half] + by_real[half:]


def kernel(
    pattern,
    inverse_root,
    inverse_one,
    inverse_two,
    inverse_three,
    lower_one,
    lower_two,
    lower_three,
    upper_one,
    upper_two,
    upper_three,
    diagonal_one,
    diagonal_two,
    diagonal_three,
    full_one,
    full_two,
    full_three,
    high_one,
    high_two,
    high_three,
    low_one,
    low_two,
    low_three,
    chain,
    join_one,
    join_two,
    joined,
    padded,
    join_diag_one,
    join_diag_two,
    send_one,
    send_two,
    send_three,
    got_one,
    got_two,
    got_three,
    turned_one,
    turned_two,
    turned_three,
    gather_send,
    gather_recv,
    join_send,
    join_recv,
    turn_send,
    turn_recv,
):
    group = lax.axis_index("group")
    me = lax.axis_index("proc")
    x_at = me // 4
    y_at = me // 2 % 2
    core = me % 2

    def proc_of(dx, dy, dc=0):
        return lax.rem(x_at + dx, 4) * 4 + lax.rem(y_at + dy, 2) * 2 + lax.rem(core + dc, 2)

    right, left = proc_of(1, 0), proc_of(3, 0)
    far, pair, sibling = proc_of(2, 0), proc_of(0, 1), proc_of(0, 0, 1)
    pair_right, pair_left, pair_far = proc_of(1, 1), proc_of(3, 1), proc_of(2, 1)

    barrier = pltpu.get_barrier_semaphore()
    for step in range(1, PROCS):
        pl.semaphore_signal(
            barrier, inc=1, device_id=(group, lax.rem(me + step, PROCS)), device_id_type=MESH
        )
    for flip in range(1, 4):
        pl.semaphore_signal(barrier, inc=1, device_id=(group ^ flip, me), device_id_type=MESH)

    def keep(level, a):
        node = group // 2 ** (3 - level)
        first = (level - 2) * 2**level + 2
        return pattern[first + node * level + a].astype(jnp.float32)

    buffers = [full_one, full_two] + [full_three.at[c] for c in range(CHUNKS)]
    highs = [high_one, high_two] + [high_three.at[c] for c in range(CHUNKS)]
    lows = [low_one, low_two] + [low_three.at[c] for c in range(CHUNKS)]

    def rows_of(proc, offset=0):
        return pl.multiple_of(proc * ROWS + offset, 8)

    own = pl.ds(rows_of(me), ROWS)

    def own_block(q):
        if q == 0:
            full_one[:, :, own, :] = jnp.zeros((2, 1, ROWS, WIDE[0]), jnp.float32)
            full_one[:, 0, own, : COLS[0]] = lower_one[:, 0] * keep(1, 0)
        elif q == 1:
            for a in range(2):
                full_two[:, a, own, :] = lower_two[:, a] * keep(2, a)
        else:
            columns = slice((q - 2) * WIDTH, (q - 1) * WIDTH)
            for a in range(3):
                full_three[q - 2, :, a, own, :] = lower_three[:, a, :, columns] * keep(3, a)

    own_block(0)
    own_block(1)
    pl.semaphore_wait(barrier, PROCS - 1 + 3)

    pending = []

    def block(chunk, part, proc, half):
        offset, count = (0, ROWS) if half is None else (half * HALF, HALF)
        return buffers[chunk].at[part, :, pl.ds(rows_of(proc, offset), count), :]

    def gather_copy(chunk, part, role, proc, to, half):
        place = block(chunk, part, proc, half)
        return pltpu.make_async_remote_copy(
            src_ref=place,
            dst_ref=place,
            send_sem=gather_send.at[chunk, part, role],
            recv_sem=gather_recv.at[chunk, part, role],
            device_id=(group, to),
            device_id_type=MESH,
        )

    def send(chunk, part, role, proc, to, half=None):
        copy = gather_copy(chunk, part, role, proc, to, half)
        copy.start()
        pending.append(copy)

    def arrive(chunk, part, role, proc, half=None):
        gather_copy(chunk, part, role, proc, sibling, half).wait_recv()

    def x_first(q, part):
        return (q, part) in X_FIRST

    def stage_a(q):
        if q > 1:
            own_block(q)
        for part in range(2):
            send(q, part, 0, me, pair)
        for part in range(2):
            send(q, part, 1, me, right)
            send(q, part, 2, me, left)
        for part in range(2):
            send(q, part, 9, me, sibling)

    def stage_b(q):
        for part in range(2):
            if not x_first(q, part):
                arrive(q, part, 0, pair)
                send(q, part, 3, pair, right)
                send(q, part, 4, pair, left)
                send(q, part, 10, pair, sibling)
        for part in range(2):
            arrive(q, part, 1, left)
            send(q, part, 5, left, right, 0)
            if x_first(q, part):
                send(q, part, 3, left, pair)
            send(q, part, 11, left, sibling)
            arrive(q, part, 2, right)
            send(q, part, 6, right, left, 1)
            if x_first(q, part):
                send(q, part, 4, right, pair)
            send(q, part, 12, right, sibling)

    def stage_c(q):
        for part in range(2):
            arrive(q, part, 5, far, 0)
            arrive(q, part, 6, far, 1)
            if x_first(q, part):
                send(q, part, 7, far, pair)
                arrive(q, part, 0, pair)
                send(q, part, 10, pair, sibling)
            send(q, part, 15, far, sibling)
        for part in range(2):
            if not x_first(q, part):
                arrive(q, part, 3, pair_left)
                send(q, part, 7, pair_left, right, 0)
                send(q, part, 13, pair_left, sibling)
                arrive(q, part, 4, pair_right)
                send(q, part, 8, pair_right, left, 1)
                send(q, part, 14, pair_right, sibling)

    def stage_d(q):
        for part in range(2):
            if x_first(q, part):
                arrive(q, part, 3, pair_left)
                send(q, part, 13, pair_left, sibling)
                arrive(q, part, 4, pair_right)
                send(q, part, 14, pair_right, sibling)
                arrive(q, part, 7, pair_far)
            else:
                arrive(q, part, 7, pair_far, 0)
                arrive(q, part, 8, pair_far, 1)
            send(q, part, 16, pair_far, sibling)

    def stage_e(q):
        flip = 1 - 2 * core
        sources = (me, pair, left, right, pair_left, pair_right, far, pair_far)
        for part in range(2):
            for at, proc in enumerate(sources):
                arrive(q, part, 9 + at, proc + flip)

    def convert(q):
        for part in range(2):
            for a in range(buffers[q].shape[1]):
                high, low = split(buffers[q][part, a])
                highs[q][part, a] = high
                lows[q][part, a] = low

    def factors(q):
        levels, width = highs[q].shape[1], highs[q].shape[3]
        return [
            ref[part].reshape(levels * S, width) for part in range(2) for ref in (highs[q], lows[q])
        ]

    def new_upper(q, level, first, last):
        depth = level * S
        rows = 2 * (last - first) * ROWS
        high = chain[0, :, first:last, :, :depth].reshape(rows, depth)
        low = chain[1, :, first:last, :, :depth].reshape(rows, depth)
        real, imag = complex_rows(high, low, *factors(q))
        shape = (last - first, ROWS, highs[q].shape[3])
        return -real.reshape(shape), -imag.reshape(shape)

    def join_copies(step, flips, ref, slot, at=()):
        copies = []
        for flip in flips:
            copy = pltpu.make_async_remote_copy(
                src_ref=ref.at[(slot, *at)],
                dst_ref=ref.at[(slot, *at)],
                send_sem=join_send.at[step, flip],
                recv_sem=join_recv.at[step, flip],
                device_id=(group ^ flip, me),
                device_id_type=MESH,
            )
            copy.start()
            copies.append(copy)
        pending.extend(copies)

    def join_waits(step, flips, ref, slot, at=()):
        for flip in flips:
            place = ref.at[(slot ^ flip, *at)]
            pltpu.make_async_remote_copy(
                src_ref=place,
                dst_ref=place,
                send_sem=join_send.at[step, flip],
                recv_sem=join_recv.at[step, flip],
                device_id=(group ^ flip, me),
                device_id_type=MESH,
            ).wait_recv()

    def squeeze(value):
        lane = lax.broadcasted_iota(jnp.int32, (HALF, 128), 1)
        rest = value[:, 128:]
        rest = jnp.where(lane < 64, rest[:HALF], pltpu.roll(rest[HALF:], 64, 1))
        return jnp.concatenate([value[:, :128], rest], axis=0)

    def stretch(value):
        rest = value[ROWS:]
        rest = jnp.concatenate([rest, pltpu.roll(rest, 64, 1)], axis=0)
        return jnp.concatenate([value[:ROWS], rest], axis=1)

    def widen(pieces):
        lane = lax.broadcasted_iota(jnp.int32, (pieces[0].shape[0], 128), 1)
        tiles = []
        for even, odd in ((pieces[0], pieces[1]), (pieces[2], pieces[3])):
            rolled = pltpu.roll(odd, 64, 1)
            tiles += [
                even[:, :128],
                jnp.where(lane < 64, even[:, 128:], rolled[:, :128]),
                rolled[:, 128:],
            ]
        return jnp.concatenate(tiles, axis=1)

    def window(real, imag, proc, base=0):
        start = proc * ROWS - base
        tile, shift = start // 128 * 128, start % 128
        count = 128 if shift + ROWS <= 128 else 256
        lane = lax.broadcasted_iota(jnp.int32, (real.shape[0], 128), 1)
        first = real[:, tile : tile + count]
        second = imag[:, tile : tile + count]
        if shift:
            first = pltpu.roll(first, count - shift, 1)[:, :128]
        if shift != ROWS:
            second = pltpu.roll(second, (count + ROWS - shift) % count, 1)[:, :128]
        return jnp.where(lane < ROWS, first[:, :128], second[:, :128])

    def pack(value):
        extra = EXTRA[value.shape[0]]
        kept = value.shape[0] - extra
        lane = lax.broadcasted_iota(jnp.int32, (extra, 128), 1)
        spare = value[kept:]
        parts = [
            jnp.where(
                lane < 2 * ROWS,
                value[t * extra : (t + 1) * extra],
                pltpu.roll(spare, 2 * ROWS - 32 * t, 1),
            )
            for t in range(3)
        ]
        return jnp.concatenate(parts + [value[3 * extra : kept]], axis=0)

    def unpack(value, count):
        extra = EXTRA[count]
        lane = lax.broadcasted_iota(jnp.int32, (extra, 128), 1)
        parts = [
            pltpu.roll(value[t * extra : (t + 1) * extra], 32 * t + 32, 1) for t in range(3)
        ]
        spare = jnp.where(lane < 32, parts[0], jnp.where(lane < 64, parts[1], parts[2]))
        return jnp.concatenate([value, spare], axis=0)

    def turn_copy(turn, source, target, to):
        return pltpu.make_async_remote_copy(
            src_ref=source.at[to],
            dst_ref=target.at[me],
            send_sem=turn_send.at[turn, to],
            recv_sem=turn_recv.at[turn, me],
            device_id=(group, to),
            device_id_type=MESH,
        )

    def turn_arrive(turn, source, target, proc):
        pltpu.make_async_remote_copy(
            src_ref=source.at[proc],
            dst_ref=target.at[proc],
            send_sem=turn_send.at[turn, proc],
            recv_sem=turn_recv.at[turn, proc],
            device_id=(group, proc),
            device_id_type=MESH,
        ).wait_recv()

    def fill(source, first, last, proc):
        rows = (last - first) * ROWS
        real = joined[0, first:last].reshape(rows, S)
        imag = joined[1, first:last].reshape(rows, S)
        source[proc] = pack(window(real, imag, proc))

    def turn_start(turn, source, target, first, last):
        for proc in range(PROCS):
            fill(source, first, last, proc)
        for step in range(1, PROCS):
            copy = turn_copy(turn, source, target, lax.rem(me + step, PROCS))
            copy.start()
            pending.append(copy)
        target[me] = source[me]

    def turn_wait(turn, source, target, turned, first, last):
        for step in range(PROCS):
            proc = lax.rem(me + PROCS - step, PROCS)
            if step:
                turn_arrive(turn, source, target, proc)
            value = unpack(target[proc], (last - first) * ROWS)
            rows = pl.ds(rows_of(proc), ROWS)
            turned[first:last, rows, :] = value.reshape(last - first, ROWS, 128)

    def turned_rows(target):
        flat = target[...].reshape(target.shape[0] * S, 128)
        return split(flat.T[: 2 * ROWS])

    def new_diagonal(q, row_high, row_low):
        return complex_rows(row_high, row_low, *factors(q))

    def put_chain(part, a, columns, value):
        high, low = split(value)
        chain[0, part, a, :, columns] = high
        chain[1, part, a, :, columns] = low

    slot_one, slot_two = lax.rem(group, 4), lax.rem(group, 2)
    flips_one, flips_two = (1, 2, 3), (1,)

    stage_a(0)
    stage_a(1)
    stage_b(0)
    stage_a(2)
    stage_c(0)
    stage_b(1)
    stage_d(0)
    stage_e(0)
    for part in range(2):
        high, low = split(inverse_root[part])
        chain[0, part, 0, :, :S] = high
        chain[1, part, 0, :, :S] = low
    convert(0)
    real, imag = new_upper(0, 1, 0, 1)
    for part, value in ((0, real), (1, imag)):
        upper_one[part] = value[:, :, : COLS[0]]
        join_one[slot_one, part] = squeeze(value[0])
    join_copies(0, flips_one, join_one, slot_one)
    stage_a(3)
    stage_c(1)
    stage_b(2)
    join_waits(0, flips_one, join_one, slot_one)
    for part in range(2):
        value = widen([stretch(join_one[j, part]) for j in range(4)])
        joined[part, 0] = value
        put_chain(part, 0, slice(S, 2 * S), value)
    turn_start(0, send_one, got_one, 0, 1)
    stage_d(1)
    stage_a(4)
    turn_wait(0, send_one, got_one, turned_one, 0, 1)
    row_high, row_low = turned_rows(turned_one)
    for part in range(2):
        rows = slice(part * ROWS, (part + 1) * ROWS)
        chain[0, part, 1, :, :S] = row_high[rows]
        chain[1, part, 1, :, :S] = row_low[rows]
    product = new_diagonal(0, row_high, row_low)
    for part in range(2):
        diagonal_one[part] = inverse_one[part] - product[part][:, : COLS[0]]
        padded[:, : COLS[0]] = diagonal_one[part]
        join_diag_one[slot_one, part] = squeeze(padded[...])
    join_copies(1, flips_one, join_diag_one, slot_one)
    stage_c(2)
    stage_b(3)
    stage_e(1)

    convert(1)

    def upper_two_rows(a):
        real, imag = new_upper(1, 2, a, a + 1)
        for part, value in ((0, real), (1, imag)):
            upper_two[part, a] = value[0]
            join_two[slot_two, part, a] = value[0]
        join_copies(2 + a, flips_two, join_two, slot_two, (slice(None), a))

    def join_two_rows(a):
        join_waits(2 + a, flips_two, join_two, slot_two, (slice(None), a))
        for part in range(2):
            for j in range(2):
                value = join_two[j, part, a]
                joined[part, a, :, j * COLS[1] : (j + 1) * COLS[1]] = value
                put_chain(part, a, slice(2 * S + j * COLS[1], 2 * S + (j + 1) * COLS[1]), value)
        turn_start(1 + a, send_two.at[a], got_two.at[a], a, a + 1)

    upper_two_rows(0)
    join_waits(1, flips_one, join_diag_one, slot_one)
    for part in range(2):
        value = widen([stretch(join_diag_one[j, part]) for j in range(4)])
        put_chain(part, 1, slice(S, 2 * S), value)
    upper_two_rows(1)
    join_two_rows(0)
    stage_d(2)
    stage_c(3)
    join_two_rows(1)
    stage_b(4)
    stage_e(2)

    def upper_three_rows(c, first, last):
        real, imag = new_upper(2 + c, 3, first, last)
        columns = slice(c * WIDTH, (c + 1) * WIDTH)
        for part, value in ((0, real), (1, imag)):
            upper_three[part, first:last, :, columns] = value
            joined[part, first:last, :, columns] = value

    def turn_three(c):
        for proc in range(c * WIDTH // ROWS, (c + 1) * WIDTH // ROWS):
            fill(send_three, 0, 3, proc)

            @pl.when(me != proc)
            def _():
                turn_copy(3, send_three, got_three, proc).start()

    convert(2)
    upper_three_rows(0, 0, 2)
    for a in range(2):
        turn_wait(1 + a, send_two.at[a], got_two.at[a], turned_two, a, a + 1)
    row_high, row_low = turned_rows(turned_two)
    for part in range(2):
        rows = slice(part * ROWS, (part + 1) * ROWS)
        chain[0, part, 2, :, : 2 * S] = row_high[rows]
        chain[1, part, 2, :, : 2 * S] = row_low[rows]
    product = new_diagonal(1, row_high, row_low)
    for part in range(2):
        value = inverse_two[part] - product[part]
        diagonal_two[part] = value
        join_diag_two[slot_two, part] = value
    join_copies(4, flips_two, join_diag_two, slot_two)
    stage_d(3)
    stage_c(4)
    stage_e(3)
    convert(3)
    upper_three_rows(1, 0, 2)
    join_waits(4, flips_two, join_diag_two, slot_two)
    for part in range(2):
        for j in range(2):
            put_chain(
                part,
                2,
                slice(2 * S + j * COLS[1], 2 * S + (j + 1) * COLS[1]),
                join_diag_two[j, part],
            )
    upper_three_rows(0, 2, 3)
    turn_three(0)
    stage_d(4)
    upper_three_rows(1, 2, 3)
    turn_three(1)
    stage_e(4)
    convert(4)
    upper_three_rows(2, 0, 3)
    turn_three(2)
    got_three[me] = send_three[me]
    turn_wait(3, send_three, got_three, turned_three, 0, 3)
    row_high, row_low = turned_rows(turned_three)
    for c in range(CHUNKS):
        columns = slice(c * WIDTH, (c + 1) * WIDTH)
        product = new_diagonal(2 + c, row_high, row_low)
        for part in range(2):
            diagonal_three[part, :, columns] = inverse_three[part, :, columns] - product[part]

    for copy in pending:
        copy.wait_send()
    for step in range(1, PROCS):
        to = lax.rem(me + step, PROCS)
        turn_copy(3, send_three, got_three, to).wait_send()


def hand_over(*refs):
    for at in range(6):
        refs[at + 6][...] = refs[at][...]


def shards(*arguments):
    f32, bf16 = jnp.float32, jnp.bfloat16
    outputs = [jax.ShapeDtypeStruct(a.shape, f32) for a in arguments[5:8] + arguments[2:5]]
    vmem = pl.BlockSpec(memory_space=pltpu.VMEM)
    fulls = [(2, 1, S, WIDE[0]), (2, 2, S, WIDE[1]), (CHUNKS, 2, 3, S, WIDTH)]
    counts = [level * ROWS - EXTRA[level * ROWS] for level in (1, 3)]
    sends = [
        (PROCS, counts[0], 128),
        (2, PROCS, counts[0], 128),
        (PROCS, counts[1], 128),
    ]
    turns = [(level, S, 128) for level in (1, 2, 3)]
    results = pl.pallas_call(
        kernel,
        out_shape=outputs,
        in_specs=[pl.BlockSpec(memory_space=pltpu.SMEM)] + [vmem] * 7,
        out_specs=[vmem] * 6,
        scratch_shapes=[pltpu.VMEM(shape, f32) for shape in fulls]
        + [pltpu.VMEM(shape, bf16) for shape in fulls]
        + [pltpu.VMEM(shape, bf16) for shape in fulls]
        + [
            pltpu.VMEM((2, 2, 3, ROWS, 3 * S), bf16),
            pltpu.VMEM((4, 2, ROWS + HALF, 128), f32),
            pltpu.VMEM((2, 2, 2, ROWS, WIDE[1]), f32),
            pltpu.VMEM((2, 3, ROWS, S), f32),
            pltpu.VMEM((ROWS, WIDE[0]), f32),
            pltpu.VMEM((4, 2, ROWS + HALF, 128), f32),
            pltpu.VMEM((2, 2, ROWS, WIDE[1]), f32),
        ]
        + [pltpu.VMEM(shape, f32) for shape in sends]
        + [pltpu.VMEM(shape, f32) for shape in sends]
        + [pltpu.VMEM(shape, f32) for shape in turns]
        + [
            pltpu.SemaphoreType.DMA((2 + CHUNKS, 2, ROLES)),
            pltpu.SemaphoreType.DMA((2 + CHUNKS, 2, ROLES)),
            pltpu.SemaphoreType.DMA((5, 4)),
            pltpu.SemaphoreType.DMA((5, 4)),
            pltpu.SemaphoreType.DMA((4, PROCS)),
            pltpu.SemaphoreType.DMA((4, PROCS)),
        ],
        compiler_params=pltpu.CompilerParams(
            collective_id=0, has_side_effects=True, vmem_limit_bytes=62 * 2**20
        ),
    )(*arguments)
    return pl.pallas_call(
        hand_over,
        out_shape=outputs,
        in_specs=[vmem] * 6,
        out_specs=[vmem] * 6,
    )(*results)


def solution(mesh):
    in_specs = (
        P(),
        P(None, "proc", None),
        P(None, "proc", "group"),
        P(None, "proc", "group"),
        P(None, "proc", "group"),
        P(None, None, "proc", "group"),
        P(None, None, "proc", "group"),
        P(None, None, "proc", "group"),
    )
    out_specs = (
        P(None, None, "proc", "group"),
        P(None, None, "proc", "group"),
        P(None, None, "proc", "group"),
        P(None, "proc", "group"),
        P(None, "proc", "group"),
        P(None, "proc", "group"),
    )
    return jax.shard_map(shards, mesh=mesh, in_specs=in_specs, out_specs=out_specs, check_vma=False)
```
